128 devices in a mesh: brick: 16 (over z, x), slab: 8 (over y, core).
Axes of the slice: x: 4, y: 4, z: 4, core: 2. Of those that a mesh axis runs over, the one named last changes fastest.
Arguments:
- traces: bfloat16 [524288, 128], P(('brick', 'slab')), may hold values from -6 to 6
- owner: int32 [524288, 1], P(('brick', 'slab')), may hold values from 0 to 127; in each aligned block of 4096 rows (0 to 4095, 4096 to 8191, ...) at most 64 rows name the same one
- patch_node: int32 [524288], P(('brick', 'slab')), may hold values from 0 to 4095
- case_weights: int32 [16], replicated, may hold values from 1 to 9
- smoothing: float32 [512, 1024], P('brick', 'slab'), may hold values from 0.3 to 3
- links: int32 [4, 512, 1024], P(None, 'brick', 'slab'), may hold values 0 or 1
- prior: float32 [4096, 1024], P('brick', 'slab'), may hold values from -6 to 6
- stiffness: float32 [4096, 1024], P('brick', 'slab'), may hold values from 0.5 to 4
Outputs:
- smoothed: float32 [512, 1024], P('brick', 'slab')
- moved: float32 [4096, 1024], P('brick', 'slab')
The draws below stay inside these ranges and needn't reach their ends.
Inputs may be any that keep to these rules, and one draw needn't show every extreme that they name: Among the 4096 face nodes of one device no owner is named more than 64 times, a bound that some block reaches.
All inputs are finite; a program needn't handle non-finite values. No bound on the sum of `links` on one device may be relied on, other than what follows from the above.
Results may differ from the reference program's by a relative error of at most 0.0003.
Values may be sent and summed in bfloat16 or wider, within the bound.
A program may use at most 64 MiB of HBM per device.

```python
import math
import jax
import jax.numpy as jnp
import numpy as np
from jax import lax

LC = 16
COMP = 8
W = 128
R_DEV = 4096
CAP = 64
TOTAL_ROWS = 524288
PW = 128
PH = 32
PN = 4096
SHEET_H = 512
SHEET_W = 1024
VH = 256
FH = 32
VOL_H = 4096
N_BRICK = 16
N_SLAB = 8


def place_ends(result, key, low, top_value):
    longest = result.shape.index(max(result.shape))
    spots = []
    for shift in (0, 1):
        where = [jax.random.randint(jax.random.fold_in(key, axis), (), 0, length) for axis, length in enumerate(result.shape)]
        where[longest] = (where[longest] + shift) % result.shape[longest]
        spots.append(tuple(where))
    return result.at[spots[0]].set(low).at[spots[1]].set(top_value)


def block_levels(key, shape, shards, smallest, top_value):
    def one(axis_at, parts):
        heights = jax.random.uniform(jax.random.fold_in(jax.random.fold_in(key, 6), axis_at), (parts,), jnp.float32, smallest / len(shards), top_value / len(shards))
        return jnp.repeat(jnp.exp(heights), shape[axis_at] // parts).reshape((-1,) + (1,) * (len(shape) - axis_at - 1))

    loudness = one(*shards[0])
    for cut in shards[1:]:
        loudness = loudness * one(*cut)
    return loudness


def shared_out(key, own, number, rows, number_of, top, limit, lean):
    ranking = jax.random.permutation(key, number_of)
    packed, usual = portions_of(number_of, rows * top, limit, lean, True), portions_of(number_of, rows * top, limit, lean, False)
    places = jnp.arange(number_of)

    def named(sizes, offset_by):
        used = int((sizes > 0).sum())
        fixed = max(1, used // 4)
        passed = fixed + (places - fixed + offset_by * (used - fixed)) % max(1, number_of - fixed)
        return jnp.zeros((number_of,), jnp.int32).at[ranking[jnp.where(places < fixed, places, passed)]].set(jnp.asarray(sizes, jnp.int32))

    sizes = jnp.where(number % 4 == 0, named(packed, number // 4), named(usual, number - number // 4 - 1))
    mixed = jax.random.permutation(jax.random.fold_in(own, 3), number_of)
    giver, receiver = mixed[0:number_of // 2 * 2:2], mixed[1:number_of // 2 * 2:2]
    room = jnp.minimum(sizes[giver] - 1, limit - sizes[receiver]) // 2
    room = jnp.where((giver == ranking[0]) | (receiver == ranking[0]) | (sizes[receiver] == 0), 0, jnp.maximum(room, 0))
    passed = jax.random.randint(jax.random.fold_in(own, 4), (number_of // 2,), 0, 1 << 20) % (room + 1)
    sizes = sizes.at[giver].add(-passed).at[receiver].add(passed)
    items = jnp.searchsorted(jnp.cumsum(sizes), jnp.arange(rows * top), side="right").astype(jnp.int32)
    grid = items.reshape(top, rows).T
    grid = grid[jax.random.permutation(jax.random.fold_in(own, 1), rows)]
    offset_by = jax.random.randint(jax.random.fold_in(own, 2), (rows, 1), 0, top)
    return jnp.take_along_axis(grid, (jnp.arange(top)[None, :] + offset_by) % top, axis=1)


def portions_of(number_of, total, reach, slope, full):
    loads = [(1 << 20) // math.isqrt(grade ** slope) + 1 for grade in range(1, number_of + 1)]
    largest = reach if full else min(reach, max(-(-total // number_of), total * loads[0] // sum(loads)))
    least = 1 if total - largest >= number_of - 1 else 0
    given, rest = [largest] + [least] * (number_of - 1), total - largest - least * (number_of - 1)
    while rest > 0:
        candidates = [i for i in range(1, number_of) if given[i] < largest] or [i for i in range(1, number_of) if given[i] < reach]
        mass, budget = sum([loads[i] for i in candidates]), rest
        for i in candidates:
            extra = min(reach - given[i], max(1, budget * loads[i] // mass), rest)
            given[i] = given[i] + extra
            rest = rest - extra
    return np.array(given)


def gaussian(stream_key, dims, spread, limit, shards=(), held_as=jnp.bfloat16):
    gain = block_levels(stream_key, dims, shards, -0.22, 0.18) if shards else 1.0
    entries = jax.random.normal(stream_key, dims, jnp.float32) * spread * gain
    return jnp.minimum(jnp.maximum(entries, -limit), limit).astype(held_as)


def setup_inputs(seed: int = 0) -> dict:
    keys = jax.random.split(jax.random.key(seed), 9)
    traces = gaussian(keys[0], (TOTAL_ROWS, W), 1.0, 6.0, ((0, 128),))
    owner_keys = jax.random.split(jax.random.fold_in(keys[1], 1), TOTAL_ROWS // R_DEV)
    owner_turns = jax.random.permutation(jax.random.fold_in(keys[1], 3), TOTAL_ROWS // R_DEV)
    owner = jax.vmap(lambda own, number: shared_out(jax.random.fold_in(keys[1], 2), own, number, R_DEV, N_BRICK * N_SLAB, 1, CAP, 2))(owner_keys, owner_turns).reshape((TOTAL_ROWS, 1))
    patch_node = place_ends(jax.random.randint(keys[2], (TOTAL_ROWS,), 0, PN), jax.random.fold_in(keys[2], 1), 0, PN - 1).astype(jnp.int32)
    case_weights = place_ends(jax.random.randint(keys[3], (LC,), 1, 10), jax.random.fold_in(keys[3], 1), 1, 9).astype(jnp.int32)
    smoothing = jnp.clip(jnp.exp(math.log(3.0) - 2.3025851 * jax.random.uniform(keys[4], (SHEET_H, SHEET_W), jnp.float32) ** block_levels(keys[4], (SHEET_H, SHEET_W), ((0, 16), (1, 8)), -0.2, 0.2)), 0.3, 3.0)
    links = place_ends((jax.random.randint(keys[5], (4, SHEET_H, SHEET_W), 0, 4) < 3).astype(jnp.int32), jax.random.fold_in(keys[5], 1), 0, 1)
    prior = gaussian(keys[6], (VOL_H, SHEET_W), 1.0, 6.0, ((0, 16), (1, 8)), jnp.float32)
    stiffness = jnp.clip(jnp.exp(math.log(4.0) - 2.0794415 * jax.random.uniform(keys[7], (VOL_H, SHEET_W), jnp.float32) ** block_levels(keys[7], (VOL_H, SHEET_W), ((0, 16), (1, 8)), -0.2, 0.2)), 0.5, 4.0)
    return {"traces": traces, "owner": owner, "patch_node": patch_node, "case_weights": case_weights, "smoothing": smoothing, "links": links, "prior": prior, "stiffness": stiffness}


def sweep_sheet(values, density, smoothing, links):
    padded = jnp.pad(values, 1)
    beside = links[0] * padded[:-2, 1:-1] + links[1] * padded[2:, 1:-1]
    beside = beside + links[2] * padded[1:-1, :-2] + links[3] * padded[1:-1, 2:]
    degree = links[0] + links[1] + links[2] + links[3]
    return (density + smoothing * beside) / (1.0 + smoothing * degree)


def reference(traces, owner, patch_node, case_weights, smoothing, links, prior, stiffness):
    count = N_BRICK * N_SLAB
    gid = (owner[:, 0] * PN + patch_node).astype(jnp.int32)
    node_traces = jax.ops.segment_sum(traces.astype(jnp.float32), gid, num_segments=count * PN)
    shaped = node_traces.reshape(count * PN, LC, COMP)
    terms = jnp.sum(shaped[:, :, :4] * shaped[:, :, 4:], axis=2)
    weights = case_weights.astype(jnp.float32)
    density = jnp.dot(terms, weights, precision=lax.Precision.HIGHEST) / jnp.sum(weights)
    sheet = density.reshape(N_BRICK, N_SLAB, PH, PW).transpose(0, 2, 1, 3).reshape(SHEET_H, SHEET_W)
    linkf = links.astype(jnp.float32)
    values = sheet
    for turn in range(2):
        values = sweep_sheet(values, sheet, smoothing, linkf)
    flat = values.reshape(N_BRICK, PH, N_SLAB, PW).transpose(0, 2, 1, 3).reshape(-1)
    shift = flat[gid]
    added = shift.reshape(N_BRICK, N_SLAB, FH, PW).transpose(0, 2, 1, 3).reshape(N_BRICK, FH, SHEET_W)
    volume = prior.reshape(N_BRICK, VH, SHEET_W)
    volume = volume.at[:, :FH, :].add(added)
    start = volume.reshape(VOL_H, SHEET_W)
    padded = jnp.pad(start, 1)
    beside = padded[:-2, 1:-1] + padded[2:, 1:-1] + padded[1:-1, :-2] + padded[1:-1, 2:]
    moved = (stiffness * start + beside) / (stiffness + 4.0)
    return values, moved
```

```python
import functools

import jax
import jax.numpy as jnp
from jax import lax
from jax.experimental import pallas as pl
from jax.experimental.pallas import tpu as pltpu
from jax.sharding import PartitionSpec as P

MESH = pl.DeviceIdType.MESH
F32 = jnp.float32
BF16 = jnp.bfloat16
I32 = jnp.int32

NB = 16
NS = 8
ND = NB * NS
ROWS = 4096
CAP = 64
W = 128
STRIDE = 37
UNSTRIDE = 45
STEPS = 8
PER = ND // STEPS
DLO = 512
CLO = 1024
CHUNK = PER * CAP


def onehot(sub, row):
    return jnp.where(sub == row, 1.0, 0.0).astype(BF16)


def lanes(x, index):
    return jnp.take_along_axis(x, index, axis=1, mode="promise_in_bounds")


def lookup(table, nrows, hi, lo):
    out = jnp.zeros(hi.shape, F32)
    for r in range(nrows):
        row = jnp.broadcast_to(table[r : r + 1, :], (8, W))
        out = jnp.where(hi == r, lanes(row, lo), out)
    return out


def kernel(
    tr_hbm, own_ref, node_ref, cw_ref, sm_ref, lk_ref, prior_ref, st_ref,
    sm_out, mv_out,
    tr, ot, plo, hib, rhs, sendbuf, recv, ints, plc, labl, r1, r2, ids, idrel, idp, nhib,
    qlo, rr, acc, sheet, vone, vtwo, hg, hv, ans, q1, q2, fin, finp, start, vu, vd, vl, vr, cl, cr, cpl, cpr,
    in_sem, tsend, trecv, lsend, lrecv, l2send, l2recv, hsend, hrecv, asend, arecv, a2send, a2recv, vsend, vrecv,
):
    b = lax.axis_index("brick")
    s = lax.axis_index("slab")
    me = b * NS + s

    bar = pltpu.get_barrier_semaphore()

    def greet(i, _):
        t = lax.rem(me + i, ND)
        pl.semaphore_signal(bar, inc=1, device_id=(t // NS, lax.rem(t, NS)), device_id_type=MESH)
        return 0

    lax.fori_loop(1, ND, greet, 0, unroll=4)
    pltpu.make_async_copy(tr_hbm, tr, in_sem).start()

    own = own_ref[...]
    order = ((own - me + ND) * UNSTRIDE) & (ND - 1)
    slabwise = (own & (NS - 1)) * NB + (own >> 3)
    ints[0] = order & 7
    ints[1] = slabwise
    sub128 = lax.broadcasted_iota(I32, (W, W), 0)

    def fill_ot(a, _):
        col = pl.ds(pl.multiple_of(a * W, W), W)
        ot[0:W, col] = onehot(sub128, ints[1, pl.ds(a, 1), :])
        return 0

    lax.fori_loop(0, 32, fill_ot, 0, unroll=4)
    upper = jnp.where(
        lax.broadcasted_iota(I32, (256, 256), 0) < lax.broadcasted_iota(I32, (256, 256), 1), 1.0, 0.0
    ).astype(BF16)
    carry = jnp.zeros((W, 1), F32)
    for k in range(16):
        block = ot[0:W, k * 256 : (k + 1) * 256]
        blockf = block.astype(F32)
        before = jnp.dot(block, upper, preferred_element_type=F32) + carry
        place = jnp.sum(before * blockf, axis=0, keepdims=True).astype(I32)
        plc[2 * k : 2 * k + 1, :] = place[:, :W]
        plc[2 * k + 1 : 2 * k + 2, :] = place[:, W:]
        carry = before[:, 255:256] + blockf[:, 255:256]

    sub64 = lax.broadcasted_iota(I32, (CAP, W), 0)

    def fill_plo(a, _):
        col = pl.ds(pl.multiple_of(a * W, W), W)
        spot = onehot(sub64, plc[pl.ds(a, 1), :])
        low = jnp.broadcast_to(ints[0, pl.ds(a, 1), :], (16, W))
        for q in range(8):
            pick = jnp.where(low == q, 1.0, 0.0).astype(BF16)
            plo[q * CAP : (q + 1) * CAP, col] = spot * jnp.concatenate([pick] * 4, axis=0)
        return 0

    lax.fori_loop(0, 32, fill_plo, 0, unroll=2)
    turned = jnp.concatenate(
        [(order >> 3).astype(F32), plc[...].astype(F32), jnp.zeros((64, W), F32)], axis=0
    ).T
    for a in range(32):
        hib[a * W : (a + 1) * W, :] = jnp.broadcast_to(turned[:, a : a + 1], (W, W)).astype(BF16)

    pl.semaphore_wait(bar, ND - 1)
    pltpu.make_async_copy(tr_hbm, tr, in_sem).wait()

    up = (lax.rem(b + NB - 1, NB), s)
    down = (lax.rem(b + 1, NB), s)
    left = (b, lax.rem(s + NS - 1, NS))
    right = (b, lax.rem(s + 1, NS))

    def rcopy(src, dst, ss, rs, dev):
        return pltpu.make_async_remote_copy(
            src_ref=src, dst_ref=dst, send_sem=ss, recv_sem=rs, device_id=dev, device_id_type=MESH
        )

    lane8 = lax.broadcasted_iota(I32, (8, W), 1)

    def early_copies():
        return [
            rcopy(prior_ref.at[pl.ds(248, 8)], vu, vsend.at[0], vrecv.at[0], down),
            rcopy(cpl, cr, vsend.at[1], vrecv.at[1], left),
            rcopy(cpr, cl, vsend.at[2], vrecv.at[2], right),
        ]

    def early():
        first = jnp.zeros((8, W), F32)
        last = jnp.zeros((8, W), F32)
        for a in range(32):
            tile = prior_ref[a * 8 : (a + 1) * 8, :]
            first = jnp.where(lane8 == a, jnp.broadcast_to(tile[:, 0:1], (8, W)), first)
            last = jnp.where(lane8 == a, jnp.broadcast_to(tile[:, W - 1 : W], (8, W)), last)
        cpl[...] = first
        cpr[...] = last
        for c in early_copies():
            c.start()

    def stage1_copy(d):
        to = lax.rem(s + d, NS)
        return rcopy(
            labl.at[pl.ds(to * NB, NB)], r1.at[pl.ds(s * NB, NB)], lsend, lrecv, (b, to)
        )

    def labels_stage1():
        node1 = node_ref[...] + 1
        ints[2] = node1 >> 6
        ints[3] = node1 & 63

        def scale(a, _):
            col = pl.ds(pl.multiple_of(a * W, W), W)
            block = ot[0:W, col]
            low = ints[3, pl.ds(a, 1), :].astype(F32)
            high = ints[2, pl.ds(a, 1), :].astype(F32)
            low = jnp.broadcast_to(low, (16, W)).astype(BF16)
            high = jnp.broadcast_to(high, (16, W)).astype(BF16)
            ot[W : 2 * W, col] = block * jnp.concatenate([low] * 8, axis=0)
            ot[0:W, col] = block * jnp.concatenate([high] * 8, axis=0)
            return 0

        lax.fori_loop(0, 32, scale, 0, unroll=2)
        spots = jnp.concatenate([plc[...].astype(F32), jnp.zeros((96, W), F32)], axis=0).T
        lane64 = (lax.broadcasted_iota(I32, (W, W), 1) & (CAP - 1)).astype(F32)
        for a in range(32):
            rhs[a * W : (a + 1) * W, 0:W] = jnp.where(
                jnp.broadcast_to(spots[:, a : a + 1], (W, W)) == lane64, 1.0, 0.0
            ).astype(BF16)
        out = jnp.dot(ot[...], rhs[:, 0:W], preferred_element_type=F32)
        labl[...] = (out[0:W, :] * 64.0 + out[W : 2 * W, :]).astype(I32)
        r1[pl.ds(pl.multiple_of(s * NB, NB), NB), :] = labl[pl.ds(pl.multiple_of(s * NB, NB), NB), :]

        def go(d, _):
            stage1_copy(d).start()
            return 0

        lax.fori_loop(1, NS, go, 0)

    def stage2_copy(d):
        to = lax.rem(b + d, NB)
        return rcopy(
            r2.at[pl.ds(to * NS, NS)], ids.at[pl.ds(b * NS, NS)], l2send, l2recv, (to, s)
        )

    def labels_stage2():
        pltpu.make_async_copy(labl.at[pl.ds(0, 7 * NB)], r1.at[pl.ds(0, 7 * NB)], lrecv).wait()
        for t in range(NB):
            r2[t * NS : (t + 1) * NS, :] = r1[pl.ds(t, NS, stride=NB), :]
        mine = pl.ds(pl.multiple_of(b * NS, NS), NS)
        ids[mine, :] = r2[mine, :]

        def go(d, _):
            stage2_copy(d).start()
            return 0

        lax.fori_loop(1, NB, go, 0)

    def trace_copy(i):
        t = lax.rem(me + STRIDE * i, ND)
        return rcopy(
            sendbuf.at[i], recv.at[i], tsend, trecv.at[i // PER], (t // NS, lax.rem(t, NS))
        )

    def dispatch(j, _):
        want0 = jnp.full((256, W), 2 * j, I32).astype(F32).astype(BF16)
        want1 = jnp.full((256, W), 2 * j + 1, I32).astype(F32).astype(BF16)

        def mask(k, _):
            rows = pl.ds(pl.multiple_of(k * 256, 256), 256)
            group = hib[rows, :]
            data = tr[rows, :]
            rhs[rows, 0:W] = jnp.where(group == want0, data, jnp.zeros_like(data))
            rhs[rows, W : 2 * W] = jnp.where(group == want1, data, jnp.zeros_like(data))
            return 0

        lax.fori_loop(0, 16, mask, 0, unroll=2)
        out = jnp.dot(plo[...], rhs[...], preferred_element_type=F32).astype(BF16)
        for h in range(2):
            sendbuf[pl.ds(PER * j + 8 * h, 8)] = out[:, h * W : (h + 1) * W].reshape(8, CAP, W)

        @pl.when(j == 0)
        def _():
            pltpu.make_async_copy(sendbuf.at[0], recv.at[0], trecv.at[0]).start()

        def go(i, _):
            trace_copy(PER * j + i).start()
            return 0

        lax.fori_loop(jnp.where(j == 0, 1, 0), PER, go, 0)

        @pl.when(j == 0)
        def _():
            labels_stage1()
            early()

        @pl.when(j == 2)
        def _():
            labels_stage2()

        return 0

    lax.fori_loop(0, STEPS, dispatch, 0)

    pltpu.make_async_copy(r2.at[pl.ds(0, 15 * NS)], ids.at[pl.ds(0, 15 * NS)], l2recv).wait()

    def reorder(i, _):
        src = lax.rem(me - STRIDE * i + ND * STRIDE, ND)
        idrel[pl.ds(i, 1), :] = ids[pl.ds(src, 1), :]
        return 0

    lax.fori_loop(0, ND, reorder, 0, unroll=8)
    lane64w = lax.broadcasted_iota(I32, (64, W), 1)
    idp[...] = jnp.where(lane64w < CAP, idrel[pl.ds(0, 64, stride=2), :], idrel[pl.ds(1, 64, stride=2), :]) - 1
    quarters = jnp.concatenate([(idp[...] >> 10).astype(F32), jnp.zeros((64, W), F32)], axis=0).T
    for a in range(64):
        nhib[a * W : (a + 1) * W, :] = jnp.broadcast_to(quarters[:, a : a + 1], (W, W)).astype(BF16)
    acc[...] = jnp.zeros_like(acc)

    def combine(k, _):
        pltpu.make_async_copy(
            sendbuf.at[pl.ds(0, PER)], recv.at[pl.ds(PER * k, PER)], trecv.at[k]
        ).wait()
        for p in range(8):
            node = idp[pl.ds(8 * k + p, 1), :] & (CLO - 1)
            spot = onehot(sub64, node & 63)
            high = jnp.broadcast_to(node >> 6, (16, W))
            for q in range(16):
                pick = jnp.where(high == q, 1.0, 0.0).astype(BF16)
                qlo[q * CAP : (q + 1) * CAP, p * W : (p + 1) * W] = spot * jnp.concatenate([pick] * 4, axis=0)

        def mask(i, _):
            rows = pl.ds(pl.multiple_of(i * 256, 256), 256)
            group = nhib[pl.ds(pl.multiple_of(k * CHUNK + i * 256, 256), 256), :]
            data = recv[pl.ds(PER * k + 4 * i, 4)].reshape(256, W)
            for h in range(4):
                rr[rows, h * W : (h + 1) * W] = jnp.where(
                    group == jnp.full((256, W), h, BF16), data, jnp.zeros_like(data)
                )
            return 0

        lax.fori_loop(0, CHUNK // 256, mask, 0)
        acc[...] += jnp.dot(qlo[...], rr[...], preferred_element_type=F32)
        return 0

    lax.fori_loop(0, STEPS, combine, 0)

    lane1 = lax.broadcasted_iota(I32, (16, W), 1)
    weights = jnp.zeros((16, W), F32)
    total = jnp.float32(0.0)
    for c in range(16):
        wc = cw_ref[c].astype(F32)
        total = total + wc
        weights = jnp.where((lane1 >> 3) == c, wc, weights)
    weights = jnp.where((lane1 & 7) < 4, weights, 0.0).astype(BF16)
    contract = (((1,), (1,)), ((), ()))
    for h in range(4):
        x = acc[:, h * W : (h + 1) * W]
        prod = x * pltpu.roll(x, W - 4, axis=1)
        coarse = prod.astype(BF16)
        fine = (prod - coarse.astype(F32)).astype(BF16)
        d = lax.dot_general(weights, coarse, contract, preferred_element_type=F32)
        d = d + lax.dot_general(weights, fine, contract, preferred_element_type=F32)
        for q in range(8):
            sheet[8 * h + q : 8 * h + q + 1, :] = d[0:1, q * W : (q + 1) * W]
    sheet[...] = sheet[...] / total

    def halo_copies(src, box, n):
        return [
            rcopy(src.at[pl.ds(0, 8)], box.at[1, pl.ds(0, 8)], hsend.at[n], hrecv.at[n], up),
            rcopy(src.at[pl.ds(24, 8)], box.at[0, pl.ds(24, 8)], hsend.at[n + 1], hrecv.at[n + 1], down),
            rcopy(src, box.at[3], hsend.at[n + 2], hrecv.at[n + 2], left),
            rcopy(src, box.at[2], hsend.at[n + 3], hrecv.at[n + 3], right),
        ]

    row32 = lax.broadcasted_iota(I32, (32, W), 0)
    lane32 = lax.broadcasted_iota(I32, (32, W), 1)
    smooth = sm_ref[...]
    link = [lk_ref[i].astype(F32) for i in range(4)]
    degree = 1.0 + smooth * (link[0] + link[1] + link[2] + link[3])

    def sweep(src, box, n):
        copies = halo_copies(src, box, n)
        for c in copies:
            c.start()
        for c in copies:
            c.wait()
        v = src[...]
        above = jnp.where(b == 0, 0.0, jnp.broadcast_to(box[0, 31:32, :], (32, W)))
        below = jnp.where(b == NB - 1, 0.0, jnp.broadcast_to(box[1, 0:1, :], (32, W)))
        before = jnp.where(s == 0, 0.0, pltpu.roll(box[2], 1, axis=1))
        after = jnp.where(s == NS - 1, 0.0, pltpu.roll(box[3], W - 1, axis=1))
        above = jnp.where(row32 == 0, above, pltpu.roll(v, 1, axis=0))
        below = jnp.where(row32 == 31, below, pltpu.roll(v, 31, axis=0))
        before = jnp.where(lane32 == 0, before, pltpu.roll(v, 1, axis=1))
        after = jnp.where(lane32 == W - 1, after, pltpu.roll(v, W - 1, axis=1))
        beside = link[0] * above + link[1] * below + link[2] * before + link[3] * after
        return (sheet[...] + smooth * beside) / degree

    vone[...] = sweep(sheet, hg, 0)
    vtwo[...] = sweep(vone, hv, 4)
    sm_out[...] = vtwo[...]

    def answer(t, _):
        rows = pl.ds(pl.multiple_of(t * 8, 8), 8)
        node = ids[rows, :] - 1
        ans[rows, :] = lookup(vtwo, 32, node >> 7, node & (W - 1))
        return 0

    lax.fori_loop(0, NB, answer, 0)

    def back1_copy(d):
        to = lax.rem(b + d, NB)
        return rcopy(ans.at[pl.ds(to * NS, NS)], q1.at[pl.ds(b * NS, NS)], asend, arecv, (to, s))

    def go1(d, _):
        back1_copy(d).start()
        return 0

    lax.fori_loop(1, NB, go1, 0)
    mine = pl.ds(pl.multiple_of(b * NS, NS), NS)
    q1[mine, :] = ans[mine, :]
    pltpu.make_async_copy(ans.at[pl.ds(0, 15 * NS)], q1.at[pl.ds(0, 15 * NS)], arecv).wait()
    for t in range(NS):
        q2[t * NB : (t + 1) * NB, :] = q1[pl.ds(t, NB, stride=NS), :]

    def back2_copy(d):
        to = lax.rem(s + d, NS)
        return rcopy(q2.at[pl.ds(to * NB, NB)], fin.at[pl.ds(s * NB, NB)], a2send, a2recv, (b, to))

    def go2(d, _):
        back2_copy(d).start()
        return 0

    lax.fori_loop(1, NS, go2, 0)
    mine = pl.ds(pl.multiple_of(s * NB, NB), NB)
    fin[mine, :] = q2[mine, :]
    pltpu.make_async_copy(q2.at[pl.ds(0, 7 * NB)], fin.at[pl.ds(0, 7 * NB)], a2recv).wait()

    finp[...] = jnp.where(lane64w < CAP, fin[pl.ds(0, 64, stride=2), :], fin[pl.ds(1, 64, stride=2), :])
    start[...] = prior_ref[...]

    def place_shift(t, _):
        rows = pl.ds(pl.multiple_of(t * 8, 8), 8)
        m = ints[1, rows, :]
        shift = lookup(finp, 64, m >> 1, ((m & 1) << 6) + plc[rows, :])
        start[rows, :] = start[rows, :] + shift
        return 0

    lax.fori_loop(0, 4, place_shift, 0)

    late = [
        rcopy(start.at[pl.ds(0, 8)], vd, vsend.at[3], vrecv.at[3], up),
        rcopy(start.at[pl.ds(0, 32)], vr, vsend.at[4], vrecv.at[4], left),
        rcopy(start.at[pl.ds(0, 32)], vl, vsend.at[5], vrecv.at[5], right),
    ]
    for c in late:
        c.start()
    for c in early_copies():
        c.wait()
    for c in late:
        c.wait()
    x = start[...]
    firsts = [pltpu.roll(vl[...], 1, axis=1)]
    lasts = [pltpu.roll(vr[...], W - 1, axis=1)]
    for a in range(4, 32):
        firsts.append(jnp.broadcast_to(cl[:, a : a + 1], (8, W)))
        lasts.append(jnp.broadcast_to(cr[:, a : a + 1], (8, W)))
    before = jnp.where(s == 0, 0.0, jnp.concatenate(firsts, axis=0))
    after = jnp.where(s == NS - 1, 0.0, jnp.concatenate(lasts, axis=0))
    above = jnp.where(b == 0, 0.0, jnp.broadcast_to(vu[7:8, :], (256, W)))
    below = jnp.where(b == NB - 1, 0.0, jnp.broadcast_to(vd[0:1, :], (256, W)))
    row256 = lax.broadcasted_iota(I32, (256, W), 0)
    lane256 = lax.broadcasted_iota(I32, (256, W), 1)
    above = jnp.where(row256 == 0, above, pltpu.roll(x, 1, axis=0))
    below = jnp.where(row256 == 255, below, pltpu.roll(x, 255, axis=0))
    before = jnp.where(lane256 == 0, before, pltpu.roll(x, 1, axis=1))
    after = jnp.where(lane256 == W - 1, after, pltpu.roll(x, W - 1, axis=1))
    stiff = st_ref[...]
    mv_out[...] = (stiff * x + (above + below + before + after)) / (stiff + 4.0)

    pltpu.make_async_copy(sendbuf.at[pl.ds(0, ND - 1)], recv.at[pl.ds(0, ND - 1)], tsend).wait()
    pltpu.make_async_copy(labl.at[pl.ds(0, 7 * NB)], r1.at[pl.ds(0, 7 * NB)], lsend).wait()
    pltpu.make_async_copy(r2.at[pl.ds(0, 15 * NS)], ids.at[pl.ds(0, 15 * NS)], l2send).wait()
    pltpu.make_async_copy(ans.at[pl.ds(0, 15 * NS)], q1.at[pl.ds(0, 15 * NS)], asend).wait()
    pltpu.make_async_copy(q2.at[pl.ds(0, 7 * NB)], fin.at[pl.ds(0, 7 * NB)], a2send).wait()


def local(traces, owner, patch_node, case_weights, smoothing, links, prior, stiffness):
    vmem = pl.BlockSpec(memory_space=pltpu.VMEM)
    V = pltpu.VMEM
    dma = pltpu.SemaphoreType.DMA
    return pl.pallas_call(
        kernel,
        out_shape=(
            jax.ShapeDtypeStruct((32, W), F32),
            jax.ShapeDtypeStruct((256, W), F32),
        ),
        in_specs=[pl.BlockSpec(memory_space=pl.ANY), vmem, vmem, pl.BlockSpec(memory_space=pltpu.SMEM)] + [vmem] * 4,
        out_specs=(vmem, vmem),
        scratch_shapes=[
            V((ROWS, W), BF16),
            V((2 * W, ROWS), BF16),
            V((DLO, ROWS), BF16),
            V((ROWS, W), BF16),
            V((ROWS, 2 * W), BF16),
            V((ND, CAP, W), BF16),
            V((ND, CAP, W), BF16),
            V((4, 32, W), I32),
            V((32, W), I32),
            V((ND, W), I32),
            V((ND, W), I32),
            V((ND, W), I32),
            V((ND, W), I32),
            V((ND, W), I32),
            V((ND // 2, W), I32),
            V((ND * CAP, W), BF16),
            V((CLO, CHUNK), BF16),
            V((CHUNK, 4 * W), BF16),
            V((CLO, 4 * W), F32),
            V((32, W), F32),
            V((32, W), F32),
            V((32, W), F32),
            V((4, 32, W), F32),
            V((4, 32, W), F32),
            V((ND, W), F32),
            V((ND, W), F32),
            V((ND, W), F32),
            V((ND, W), F32),
            V((ND // 2, W), F32),
            V((256, W), F32),
            V((8, W), F32),
            V((8, W), F32),
            V((32, W), F32),
            V((32, W), F32),
            V((8, W), F32),
            V((8, W), F32),
            V((8, W), F32),
            V((8, W), F32),
            dma, dma, dma((STEPS,)), dma, dma, dma, dma, dma((8,)), dma((8,)), dma, dma, dma, dma, dma((6,)), dma((6,)),
        ],
        compiler_params=pltpu.CompilerParams(
            collective_id=0, has_side_effects=True, vmem_limit_bytes=56 << 20
        ),
    )(
        traces, owner.reshape(32, W), patch_node.reshape(32, W), case_weights, smoothing, links, prior, stiffness
    )


def solution(mesh):
    in_specs = (
        P(("brick", "slab"), None),
        P(("brick", "slab"), None),
        P(("brick", "slab")),
        P(),
        P("brick", "slab"),
        P(None, "brick", "slab"),
        P("brick", "slab"),
        P("brick", "slab"),
    )
    out_specs = (P("brick", "slab"), P("brick", "slab"))
    return jax.shard_map(local, mesh=mesh, in_specs=in_specs, out_specs=out_specs, check_vma=False)
```

```python
import functools

import jax
import jax.numpy as jnp
from jax import lax
from jax.experimental import pallas as pl
from jax.experimental.pallas import tpu as pltpu
from jax.sharding import PartitionSpec as P

MESH = pl.DeviceIdType.MESH
F32 = jnp.float32
BF16 = jnp.bfloat16
I32 = jnp.int32

NB = 16
NS = 8
ND = NB * NS
ROWS = 4096
CAP = 64
W = 128
STRIDE = 37
UNSTRIDE = 45
BACK = 21
STEPS = 8
PER = ND // STEPS
DLO = 512
CLO = 1024
CHUNK = PER * CAP


def onehot(sub, row):
    return jnp.where(sub == row, 1.0, 0.0).astype(BF16)


def lanes(x, index):
    return jnp.take_along_axis(x, index, axis=1, mode="promise_in_bounds")


def lookup(table, nrows, hi, lo):
    out = jnp.zeros(hi.shape, F32)
    for r in range(nrows):
        row = jnp.broadcast_to(table[r : r + 1, :], (8, W))
        out = jnp.where(hi == r, lanes(row, lo), out)
    return out


def kernel(
    tr_hbm, own_ref, node_ref, cw_ref, sm_ref, lk_ref, prior_ref, st_ref,
    sm_out, mv_out,
    tr, ot, plo, hib, rhs, sendbuf, recv, ints, plc, labl, r1, r2, ids, idrel, idp, nhib,
    qlo, acc, sheet, vtwo, sides, ends, pairs, ans, msg, back, mine3, other3, tables, codes, eu, ed, el, er, vu, vd, vl, vr,
    in_sem, tsend, trecv, lsend, lrecv, l2send, l2recv, hsend, hrecv, asend, arecv, csend, crecv, vsend, vrecv,
):
    b = lax.axis_index("brick")
    s = lax.axis_index("slab")
    me = b * NS + s

    bar = pltpu.get_barrier_semaphore()

    def greet(i, _):
        t = lax.rem(me + i, ND)
        pl.semaphore_signal(bar, inc=1, device_id=(t // NS, lax.rem(t, NS)), device_id_type=MESH)
        return 0

    lax.fori_loop(1, ND, greet, 0, unroll=4)
    pltpu.make_async_copy(tr_hbm, tr, in_sem).start()

    own = own_ref[...]
    order = ((own - me + ND) * UNSTRIDE - 1) & (ND - 1)
    slabwise = (own & (NS - 1)) * NB + (own >> 3)
    ints[0] = order & 7
    ints[1] = slabwise
    sub128 = lax.broadcasted_iota(I32, (W, W), 0)

    def fill_ot(a, _):
        col = pl.ds(pl.multiple_of(a * W, W), W)
        ot[0:W, col] = onehot(sub128, ints[1, pl.ds(a, 1), :])
        return 0

    lax.fori_loop(0, 32, fill_ot, 0, unroll=4)
    upper = jnp.where(
        lax.broadcasted_iota(I32, (256, 256), 0) < lax.broadcasted_iota(I32, (256, 256), 1), 1.0, 0.0
    ).astype(BF16)
    carry = jnp.zeros((W, 1), F32)
    for k in range(16):
        block = ot[0:W, k * 256 : (k + 1) * 256]
        blockf = block.astype(F32)
        before = jnp.dot(block, upper, preferred_element_type=F32) + carry
        place = jnp.sum(before * blockf, axis=0, keepdims=True).astype(I32)
        plc[2 * k : 2 * k + 1, :] = place[:, :W]
        plc[2 * k + 1 : 2 * k + 2, :] = place[:, W:]
        carry = before[:, 255:256] + blockf[:, 255:256]

    codes[...] = own * CAP + plc[...]

    sub64 = lax.broadcasted_iota(I32, (CAP, W), 0)

    def fill_plo(a, _):
        col = pl.ds(pl.multiple_of(a * W, W), W)
        spot = onehot(sub64, plc[pl.ds(a, 1), :])
        low = jnp.broadcast_to(ints[0, pl.ds(a, 1), :], (16, W))
        for q in range(8):
            pick = jnp.where(low == q, 1.0, 0.0).astype(BF16)
            plo[q * CAP : (q + 1) * CAP, col] = spot * jnp.concatenate([pick] * 4, axis=0)
        return 0

    lax.fori_loop(0, 32, fill_plo, 0, unroll=2)
    turned = jnp.concatenate(
        [(order >> 3).astype(F32), plc[...].astype(F32), jnp.zeros((64, W), F32)], axis=0
    ).T
    for a in range(32):
        hib[a * W : (a + 1) * W, :] = jnp.broadcast_to(turned[:, a : a + 1], (W, W)).astype(BF16)

    pltpu.make_async_copy(tr_hbm, tr, in_sem).wait()

    up = (lax.rem(b + NB - 1, NB), s)
    down = (lax.rem(b + 1, NB), s)
    left = (b, lax.rem(s + NS - 1, NS))
    right = (b, lax.rem(s + 1, NS))

    def rcopy(src, dst, ss, rs, dev):
        return pltpu.make_async_remote_copy(
            src_ref=src, dst_ref=dst, send_sem=ss, recv_sem=rs, device_id=dev, device_id_type=MESH
        )

    lane8 = lax.broadcasted_iota(I32, (8, W), 1)

    def early_copies():
        return [
            rcopy(eu, vd, vsend.at[0], vrecv.at[0], up),
            rcopy(ed, vu, vsend.at[1], vrecv.at[1], down),
            rcopy(el, vr, vsend.at[2], vrecv.at[2], left),
            rcopy(er, vl, vsend.at[3], vrecv.at[3], right),
        ]

    def early():
        eu[...] = jnp.zeros_like(eu)
        ed[...] = jnp.zeros_like(ed)
        eu[0:1, :] = sm_ref[0:1, :]
        ed[0:1, :] = sm_ref[31:32, :]
        for k in range(4):
            eu[k + 1 : k + 2, :] = lk_ref[k, 0:1, :].astype(F32)
            ed[k + 1 : k + 2, :] = lk_ref[k, 31:32, :].astype(F32)
        eu[5:6, :] = codes[0:1, :].astype(F32)
        eu[6:7, :] = prior_ref[0:1, :]
        ed[5:6, :] = prior_ref[255:256, :]
        columns = [prior_ref[a * 8 : (a + 1) * 8, :] for a in range(32)]
        columns += [sm_ref[a * 8 : (a + 1) * 8, :] for a in range(4)]
        for k in range(4):
            columns += [lk_ref[k, a * 8 : (a + 1) * 8, :].astype(F32) for a in range(4)]
        columns += [codes[a * 8 : (a + 1) * 8, :].astype(F32) for a in range(4)]
        first = jnp.zeros((8, W), F32)
        last = jnp.zeros((8, W), F32)
        for a, tile in enumerate(columns):
            first = jnp.where(lane8 == a, jnp.broadcast_to(tile[:, 0:1], (8, W)), first)
            last = jnp.where(lane8 == a, jnp.broadcast_to(tile[:, W - 1 : W], (8, W)), last)
        el[...] = first
        er[...] = last
        for c in early_copies():
            c.start()

    def stage1_copy(d):
        to = lax.rem(s + d, NS)
        return rcopy(
            labl.at[pl.ds(to * NB, NB)], r1.at[pl.ds(s * NB, NB)], lsend, lrecv, (b, to)
        )

    def labels_stage1():
        node1 = node_ref[...] + 1
        ints[2] = node1 >> 6
        ints[3] = node1 & 63

        def scale(a, _):
            col = pl.ds(pl.multiple_of(a * W, W), W)
            block = ot[0:W, col]
            low = ints[3, pl.ds(a, 1), :].astype(F32)
            high = ints[2, pl.ds(a, 1), :].astype(F32)
            low = jnp.broadcast_to(low, (16, W)).astype(BF16)
            high = jnp.broadcast_to(high, (16, W)).astype(BF16)
            ot[W : 2 * W, col] = block * jnp.concatenate([low] * 8, axis=0)
            ot[0:W, col] = block * jnp.concatenate([high] * 8, axis=0)
            return 0

        lax.fori_loop(0, 32, scale, 0, unroll=2)
        spots = jnp.concatenate([plc[...].astype(F32), jnp.zeros((96, W), F32)], axis=0).T
        lane64 = (lax.broadcasted_iota(I32, (W, W), 1) & (CAP - 1)).astype(F32)
        for a in range(32):
            rhs[a * W : (a + 1) * W, 0:W] = jnp.where(
                jnp.broadcast_to(spots[:, a : a + 1], (W, W)) == lane64, 1.0, 0.0
            ).astype(BF16)
        out = jnp.dot(ot[...], rhs[:, 0:W], preferred_element_type=F32)
        labl[...] = (out[0:W, :] * 64.0 + out[W : 2 * W, :]).astype(I32)
        r1[pl.ds(pl.multiple_of(s * NB, NB), NB), :] = labl[pl.ds(pl.multiple_of(s * NB, NB), NB), :]

        pl.semaphore_wait(bar, ND - 1)

        def go(d, _):
            stage1_copy(d).start()
            return 0

        lax.fori_loop(1, NS, go, 0)

    def stage2_copy(d):
        to = lax.rem(b + d, NB)
        return rcopy(
            r2.at[pl.ds(to * NS, NS)], ids.at[pl.ds(b * NS, NS)], l2send, l2recv, (to, s)
        )

    def labels_stage2():
        pltpu.make_async_copy(labl.at[pl.ds(0, 7 * NB)], r1.at[pl.ds(0, 7 * NB)], lrecv).wait()
        for t in range(NB):
            r2[t * NS : (t + 1) * NS, :] = r1[pl.ds(t, NS, stride=NB), :]
        mine = pl.ds(pl.multiple_of(b * NS, NS), NS)
        ids[mine, :] = r2[mine, :]

        def go(d, _):
            stage2_copy(d).start()
            return 0

        lax.fori_loop(1, NB, go, 0)

    def trace_copy(i):
        t = lax.rem(me + STRIDE * (i + 1), ND)
        return rcopy(
            sendbuf.at[i], recv.at[i], tsend, trecv.at[i // PER], (t // NS, lax.rem(t, NS))
        )

    def fill_step(j):
        group = hib[...]
        data = tr[...]
        masked = [
            jnp.where(group == jnp.full((ROWS, W), 2 * j + h, I32).astype(F32).astype(BF16), data, jnp.zeros_like(data))
            for h in range(2)
        ]
        out = jnp.dot(plo[...], jnp.concatenate(masked, axis=1), preferred_element_type=F32).astype(BF16)
        for h in range(2):
            sendbuf[pl.ds(PER * j + 8 * h, 8)] = out[:, h * W : (h + 1) * W].reshape(8, CAP, W)

    def dispatch(j, _):
        def go(i, _):
            trace_copy(PER * (j - 1) + i).start()
            return 0

        lax.fori_loop(0, PER, go, 0)
        fill_step(j)

        @pl.when(j == 1)
        def _():
            labels_stage2()

        @pl.when(j == 4)
        def _():
            early()

        return 0

    labels_stage1()
    fill_step(0)
    lax.fori_loop(1, STEPS, dispatch, 0)

    def last(i, _):
        trace_copy(PER * (STEPS - 1) + i).start()
        return 0

    lax.fori_loop(0, PER - 1, last, 0)
    pltpu.make_async_copy(sendbuf.at[ND - 1], recv.at[ND - 1], trecv.at[STEPS - 1]).start()

    pltpu.make_async_copy(r2.at[pl.ds(0, 15 * NS)], ids.at[pl.ds(0, 15 * NS)], l2recv).wait()

    def reorder(i, _):
        src = lax.rem(me - STRIDE * (i + 1) + ND * STRIDE, ND)
        idrel[pl.ds(i, 1), :] = ids[pl.ds(src, 1), :]
        return 0

    lax.fori_loop(0, ND, reorder, 0, unroll=8)
    lane64w = lax.broadcasted_iota(I32, (64, W), 1)
    pairs[...] = jnp.where(lane64w < CAP, ids[pl.ds(0, 64, stride=2), :], ids[pl.ds(1, 64, stride=2), :]) - 1
    idp[...] = jnp.where(lane64w < CAP, idrel[pl.ds(0, 64, stride=2), :], idrel[pl.ds(1, 64, stride=2), :]) - 1
    quarters = jnp.concatenate([(idp[...] >> 10).astype(F32), jnp.zeros((64, W), F32)], axis=0).T
    for a in range(64):
        nhib[a * W : (a + 1) * W, :] = jnp.broadcast_to(quarters[:, a : a + 1], (W, W)).astype(BF16)
    acc[...] = jnp.zeros_like(acc)

    def combine(k, _):
        pltpu.make_async_copy(
            sendbuf.at[pl.ds(0, PER)], recv.at[pl.ds(PER * k, PER)], trecv.at[k]
        ).wait()
        for p in range(8):
            node = idp[pl.ds(8 * k + p, 1), :] & (CLO - 1)
            spot = onehot(sub64, node & 63)
            high = jnp.broadcast_to(node >> 6, (16, W))
            for q in range(16):
                pick = jnp.where(high == q, 1.0, 0.0).astype(BF16)
                qlo[q * CAP : (q + 1) * CAP, p * W : (p + 1) * W] = spot * jnp.concatenate([pick] * 4, axis=0)

        group = nhib[pl.ds(pl.multiple_of(k * CHUNK, CHUNK), CHUNK), :]
        data = recv[pl.ds(PER * k, PER)].reshape(CHUNK, W)
        masked = [
            jnp.where(group == jnp.full((CHUNK, W), h, BF16), data, jnp.zeros_like(data)) for h in range(4)
        ]
        acc[...] += jnp.dot(qlo[...], jnp.concatenate(masked, axis=1), preferred_element_type=F32)
        return 0

    lax.fori_loop(0, STEPS, combine, 0)

    lane1 = lax.broadcasted_iota(I32, (16, W), 1)
    weights = jnp.zeros((16, W), F32)
    total = jnp.float32(0.0)
    for c in range(16):
        wc = cw_ref[c].astype(F32)
        total = total + wc
        weights = jnp.where((lane1 >> 3) == c, wc, weights)
    weights = jnp.where((lane1 & 7) < 4, weights, 0.0).astype(BF16)
    contract = (((1,), (1,)), ((), ()))
    for h in range(4):
        x = acc[:, h * W : (h + 1) * W]
        prod = x * pltpu.roll(x, W - 4, axis=1)
        coarse = prod.astype(BF16)
        fine = (prod - coarse.astype(F32)).astype(BF16)
        d = lax.dot_general(weights, coarse, contract, preferred_element_type=F32)
        d = d + lax.dot_general(weights, fine, contract, preferred_element_type=F32)
        for q in range(8):
            sheet[8 * h + q : 8 * h + q + 1, :] = d[0:1, q * W : (q + 1) * W]
    sheet[...] = sheet[...] / total

    upleft = (lax.rem(b + NB - 1, NB), lax.rem(s + NS - 1, NS))
    upright = (lax.rem(b + NB - 1, NB), lax.rem(s + 1, NS))
    downleft = (lax.rem(b + 1, NB), lax.rem(s + NS - 1, NS))
    downright = (lax.rem(b + 1, NB), lax.rem(s + 1, NS))
    top = sheet.at[pl.ds(0, 8)]
    bottom = sheet.at[pl.ds(24, 8)]
    swaps = [
        rcopy(top, ends.at[5], hsend.at[5], hrecv.at[5], upleft),
        rcopy(top, ends.at[4], hsend.at[4], hrecv.at[4], upright),
        rcopy(bottom, ends.at[3], hsend.at[3], hrecv.at[3], downleft),
        rcopy(bottom, ends.at[2], hsend.at[2], hrecv.at[2], downright),
        rcopy(top, ends.at[1], hsend.at[1], hrecv.at[1], up),
        rcopy(bottom, ends.at[0], hsend.at[0], hrecv.at[0], down),
        rcopy(sheet, sides.at[1], hsend.at[6], hrecv.at[6], left),
        rcopy(sheet, sides.at[0], hsend.at[7], hrecv.at[7], right),
    ]
    for c in swaps:
        c.start()
    row32 = lax.broadcasted_iota(I32, (32, W), 0)
    lane32 = lax.broadcasted_iota(I32, (32, W), 1)
    lane1r = lax.broadcasted_iota(I32, (1, W), 1)
    smooth = sm_ref[...]
    link = [lk_ref[i].astype(F32) for i in range(4)]
    no_up, no_down, no_left, no_right = b == 0, b == NB - 1, s == 0, s == NS - 1

    def relax(v, smooth, link, above, below, before, after):
        beside = link[0] * above + link[1] * below + link[2] * before + link[3] * after
        return (v + smooth * beside) / (1.0 + smooth * (link[0] + link[1] + link[2] + link[3]))

    def column(tile, k):
        parts = [jnp.broadcast_to(tile[:, 32 + 4 * k + t : 33 + 4 * k + t], (8, W)) for t in range(4)]
        return jnp.concatenate(parts, axis=0)

    for c in early_copies():
        c.wait()
    coef_left = [column(vl[...], k) for k in range(5)]
    coef_right = [column(vr[...], k) for k in range(5)]
    g = sheet[...]
    for c in swaps:
        c.wait()
    gu6 = jnp.where(no_up, 0.0, ends[0, 6:7, :])
    gu7 = jnp.where(no_up, 0.0, ends[0, 7:8, :])
    gd0 = jnp.where(no_down, 0.0, ends[1, 0:1, :])
    gd1 = jnp.where(no_down, 0.0, ends[1, 1:2, :])
    gul = jnp.where(no_up | no_left, 0.0, ends[2, 7:8, :])
    gur = jnp.where(no_up | no_right, 0.0, ends[3, 7:8, :])
    gdl = jnp.where(no_down | no_left, 0.0, ends[4, 0:1, :])
    gdr = jnp.where(no_down | no_right, 0.0, ends[5, 0:1, :])
    gl = jnp.where(no_left, 0.0, sides[0])
    gr = jnp.where(no_right, 0.0, sides[1])

    def shifted(v, above, below, before, after):
        return (
            jnp.where(row32 == 0, above, pltpu.roll(v, 1, axis=0)),
            jnp.where(row32 == 31, below, pltpu.roll(v, 31, axis=0)),
            jnp.where(lane32 == 0, pltpu.roll(before, 1, axis=1), pltpu.roll(v, 1, axis=1)),
            jnp.where(lane32 == W - 1, pltpu.roll(after, W - 1, axis=1), pltpu.roll(v, W - 1, axis=1)),
        )

    def shifted_row(v, before, after):
        return (
            jnp.where(lane1r == 0, pltpu.roll(before, 1, axis=1), pltpu.roll(v, 1, axis=1)),
            jnp.where(lane1r == W - 1, pltpu.roll(after, W - 1, axis=1), pltpu.roll(v, W - 1, axis=1)),
        )

    one = relax(g, smooth, link, *shifted(g, gu7, gd0, gl, gr))
    one_up = relax(
        gu7, vu[0:1, :], [vu[k : k + 1, :] for k in range(1, 5)], gu6, g[0:1, :], *shifted_row(gu7, gul, gur)
    )
    one_down = relax(
        gd0, vd[0:1, :], [vd[k : k + 1, :] for k in range(1, 5)], g[31:32, :], gd1, *shifted_row(gd0, gdl, gdr)
    )
    one_left = relax(gl, coef_left[0], coef_left[1:], *shifted(gl, gul, gdl, gl, g))
    one_right = relax(gr, coef_right[0], coef_right[1:], *shifted(gr, gur, gdr, g, gr))
    one_up = jnp.where(no_up, 0.0, one_up)
    one_down = jnp.where(no_down, 0.0, one_down)
    one_left = jnp.where(no_left, 0.0, one_left)
    one_right = jnp.where(no_right, 0.0, one_right)
    beside = shifted(one, one_up, one_down, one_left, one_right)
    sumside = link[0] * beside[0] + link[1] * beside[1] + link[2] * beside[2] + link[3] * beside[3]
    two = (g + smooth * sumside) / (1.0 + smooth * (link[0] + link[1] + link[2] + link[3]))
    vtwo[...] = two
    sm_out[...] = two

    def answer(t, _):
        rows = pl.ds(pl.multiple_of(t * 8, 8), 8)
        node = pairs[rows, :]
        ans[rows, :] = lookup(vtwo, 32, node >> 7, node & (W - 1))
        return 0

    lax.fori_loop(0, 8, answer, 0)
    pair = ans[...]
    msg[pl.ds(0, 64, stride=8), :] = pair
    msg[pl.ds(1, 64, stride=8), :] = pltpu.roll(pair, 60, axis=0)
    msg[pl.ds(2, 64, stride=8), :] = jnp.where(
        lane64w < CAP, pltpu.roll(pair, 63, axis=0), pltpu.roll(pair, 1, axis=0)
    )
    core = lax.rem(s, 2)
    chip = b * 4 + s // 2

    def back_copy(i):
        t = lax.rem(chip + BACK * i, ND // 2)
        return rcopy(
            msg.at[pl.ds(t * 8, 8)], back.at[pl.ds(chip * 8, 8)], asend, arecv, (t // 4, 2 * lax.rem(t, 4) + core)
        )

    def go1(i, _):
        back_copy(i).start()
        return 0

    lax.fori_loop(1, ND // 2, go1, 0)
    here = pl.ds(pl.multiple_of(chip * 8, 8), 8)
    back[here, :] = msg[here, :]
    pltpu.make_async_copy(msg.at[pl.ds(0, 63 * 8)], back.at[pl.ds(0, 63 * 8)], arecv).wait()
    for k in range(3):
        mine3[k] = back[pl.ds(k, 64, stride=8), :]
    swap = rcopy(mine3, other3, csend, crecv, (b, s + 1 - 2 * core))
    swap.start()
    swap.wait()
    def halves(k, half):
        own_part, other_part = mine3[k], other3[k]
        even = jnp.where(core == 0, own_part, other_part)
        odd = jnp.where(core == 0, other_part, own_part)
        even = jnp.where(half == 0, even, pltpu.roll(even, CAP, axis=1))
        odd = jnp.where(half == 1, odd, pltpu.roll(odd, CAP, axis=1))
        return jnp.where(lane64w < CAP, even, odd)

    partner_table = halves(0, 1 - core)
    far_table = halves(2, 1 - core)
    tables[0] = halves(0, core)
    tables[1] = halves(1, core)
    tables[2] = jnp.where(core == 0, far_table, partner_table)
    tables[3] = jnp.where(core == 0, partner_table, far_table)

    def answered(k, code):
        return lookup(tables.at[k], 64, code >> 7, code & (W - 1))

    shift = jnp.concatenate([answered(0, codes[a * 8 : (a + 1) * 8, :]) for a in range(4)], axis=0)
    shift_down = answered(1, vd[...].astype(I32))[5:6, :]
    lanes_late = lane8 < 4
    edge_left = vl[...]
    edge_right = vr[...]
    edge_left = edge_left + jnp.where(
        lanes_late, pltpu.roll(answered(2, edge_left.astype(I32)), W - 52, axis=1), 0.0
    )
    edge_right = edge_right + jnp.where(
        lanes_late, pltpu.roll(answered(3, edge_right.astype(I32)), W - 52, axis=1), 0.0
    )
    x = jnp.concatenate([prior_ref[0:32, :] + shift, prior_ref[32:256, :]], axis=0)
    before = jnp.concatenate([jnp.broadcast_to(edge_left[:, a : a + 1], (8, W)) for a in range(32)], axis=0)
    after = jnp.concatenate([jnp.broadcast_to(edge_right[:, a : a + 1], (8, W)) for a in range(32)], axis=0)
    before = jnp.where(no_left, 0.0, before)
    after = jnp.where(no_right, 0.0, after)
    above = jnp.where(no_up, 0.0, vu[5:6, :])
    below = jnp.where(no_down, 0.0, vd[6:7, :] + shift_down)
    row256 = lax.broadcasted_iota(I32, (256, W), 0)
    lane256 = lax.broadcasted_iota(I32, (256, W), 1)
    above = jnp.where(row256 == 0, above, pltpu.roll(x, 1, axis=0))
    below = jnp.where(row256 == 255, below, pltpu.roll(x, 255, axis=0))
    before = jnp.where(lane256 == 0, before, pltpu.roll(x, 1, axis=1))
    after = jnp.where(lane256 == W - 1, after, pltpu.roll(x, W - 1, axis=1))
    stiff = st_ref[...]
    mv_out[...] = (stiff * x + (above + below + before + after)) / (stiff + 4.0)

    pltpu.make_async_copy(sendbuf.at[pl.ds(0, ND - 1)], recv.at[pl.ds(0, ND - 1)], tsend).wait()
    pltpu.make_async_copy(labl.at[pl.ds(0, 7 * NB)], r1.at[pl.ds(0, 7 * NB)], lsend).wait()
    pltpu.make_async_copy(r2.at[pl.ds(0, 15 * NS)], ids.at[pl.ds(0, 15 * NS)], l2send).wait()
    pltpu.make_async_copy(msg.at[pl.ds(0, 63 * 8)], back.at[pl.ds(0, 63 * 8)], asend).wait()


def local(traces, owner, patch_node, case_weights, smoothing, links, prior, stiffness):
    vmem = pl.BlockSpec(memory_space=pltpu.VMEM)
    V = pltpu.VMEM
    dma = pltpu.SemaphoreType.DMA
    return pl.pallas_call(
        kernel,
        out_shape=(
            jax.ShapeDtypeStruct((32, W), F32),
            jax.ShapeDtypeStruct((256, W), F32),
        ),
        in_specs=[pl.BlockSpec(memory_space=pl.ANY), vmem, vmem, pl.BlockSpec(memory_space=pltpu.SMEM)] + [vmem] * 4,
        out_specs=(vmem, vmem),
        scratch_shapes=[
            V((ROWS, W), BF16),
            V((2 * W, ROWS), BF16),
            V((DLO, ROWS), BF16),
            V((ROWS, W), BF16),
            V((ROWS, 2 * W), BF16),
            V((ND, CAP, W), BF16),
            V((ND, CAP, W), BF16),
            V((4, 32, W), I32),
            V((32, W), I32),
            V((ND, W), I32),
            V((ND, W), I32),
            V((ND, W), I32),
            V((ND, W), I32),
            V((ND, W), I32),
            V((ND // 2, W), I32),
            V((ND * CAP, W), BF16),
            V((CLO, CHUNK), BF16),
            V((CLO, 4 * W), F32),
            V((32, W), F32),
            V((32, W), F32),
            V((2, 32, W), F32),
            V((6, 8, W), F32),
            V((ND // 2, W), I32),
            V((ND // 2, W), F32),
            V((ND * 4, W), F32),
            V((ND * 4, W), F32),
            V((3, ND // 2, W), F32),
            V((3, ND // 2, W), F32),
            V((4, ND // 2, W), F32),
            V((32, W), I32),
            V((8, W), F32),
            V((8, W), F32),
            V((8, W), F32),
            V((8, W), F32),
            V((8, W), F32),
            V((8, W), F32),
            V((8, W), F32),
            V((8, W), F32),
            dma, dma, dma((STEPS,)), dma, dma, dma, dma, dma((8,)), dma((8,)), dma, dma, dma, dma, dma((4,)), dma((4,)),
        ],
        compiler_params=pltpu.CompilerParams(
            collective_id=0, has_side_effects=True, vmem_limit_bytes=56 << 20
        ),
    )(
        traces, owner.reshape(32, W), patch_node.reshape(32, W), case_weights, smoothing, links, prior, stiffness
    )


def solution(mesh):
    in_specs = (
        P(("brick", "slab"), None),
        P(("brick", "slab"), None),
        P(("brick", "slab")),
        P(),
        P("brick", "slab"),
        P(None, "brick", "slab"),
        P("brick", "slab"),
        P("brick", "slab"),
    )
    out_specs = (P("brick", "slab"), P("brick", "slab"))
    return jax.shard_map(local, mesh=mesh, in_specs=in_specs, out_specs=out_specs, check_vma=False)
```

```python
import functools

import jax
import jax.numpy as jnp
from jax import lax
from jax.experimental import pallas as pl
from jax.experimental.pallas import tpu as pltpu
from jax.sharding import PartitionSpec as P

MESH = pl.DeviceIdType.MESH
F32 = jnp.float32
BF16 = jnp.bfloat16
I32 = jnp.int32

NB = 16
NS = 8
ND = NB * NS
ROWS = 4096
CAP = 64
W = 128
STRIDE = 29
UNSTRIDE = 53
STEPS = 8
PER = ND // STEPS
DLO = 512
CLO = 1024
CHUNK = PER * CAP


def onehot(sub, row):
    return jnp.where(sub == row, 1.0, 0.0).astype(BF16)


def lanes(x, index):
    return jnp.take_along_axis(x, index, axis=1, mode="promise_in_bounds")


def lookup(table, nrows, hi, lo):
    out = jnp.zeros(hi.shape, F32)
    for r in range(nrows):
        row = jnp.broadcast_to(table[r : r + 1, :], (8, W))
        out = jnp.where(hi == r, lanes(row, lo), out)
    return out


def kernel(
    tr_hbm, own_ref, node_ref, cw_ref, sm_ref, lk_ref, prior_ref, st_ref,
    sm_out, mv_out,
    tr, ot, plo, hib, rhs, sendbuf, recv, ints, plc, labl, r1, r2, ids, idrel, idp, nhib,
    qlo, acc, sheet, vtwo, sides, ends, pairs, ans, msg, back, mine3, other3, tables, codes, eu, ed, el, er, vu, vd, vl, vr,
    in_sem, tsend, trecv, lsend, lrecv, l2send, l2recv, hsend, hrecv, asend, arecv, csend, crecv, vsend, vrecv,
):
    b = lax.axis_index("brick")
    s = lax.axis_index("slab")
    me = b * NS + s

    bar = pltpu.get_barrier_semaphore()

    def greet(i, _):
        t = lax.rem(me + i, ND)
        pl.semaphore_signal(bar, inc=1, device_id=(t // NS, lax.rem(t, NS)), device_id_type=MESH)
        return 0

    lax.fori_loop(1, ND, greet, 0, unroll=4)
    pltpu.make_async_copy(tr_hbm, tr, in_sem).start()

    own = own_ref[...]
    order = ((own - me + ND) * UNSTRIDE - 1) & (ND - 1)
    slabwise = (own & (NS - 1)) * NB + (own >> 3)
    ints[0] = order & 7
    ints[1] = slabwise
    sub128 = lax.broadcasted_iota(I32, (W, W), 0)

    def fill_ot(a, _):
        col = pl.ds(pl.multiple_of(a * W, W), W)
        ot[0:W, col] = onehot(sub128, ints[1, pl.ds(a, 1), :])
        return 0

    lax.fori_loop(0, 32, fill_ot, 0, unroll=4)
    upper = jnp.where(
        lax.broadcasted_iota(I32, (256, 256), 0) < lax.broadcasted_iota(I32, (256, 256), 1), 1.0, 0.0
    ).astype(BF16)
    carry = jnp.zeros((W, 1), F32)
    for k in range(16):
        block = ot[0:W, k * 256 : (k + 1) * 256]
        blockf = block.astype(F32)
        before = jnp.dot(block, upper, preferred_element_type=F32) + carry
        place = jnp.sum(before * blockf, axis=0, keepdims=True).astype(I32)
        plc[2 * k : 2 * k + 1, :] = place[:, :W]
        plc[2 * k + 1 : 2 * k + 2, :] = place[:, W:]
        carry = before[:, 255:256] + blockf[:, 255:256]

    codes[...] = own * CAP + plc[...]

    sub64 = lax.broadcasted_iota(I32, (CAP, W), 0)

    def fill_plo(a, _):
        col = pl.ds(pl.multiple_of(a * W, W), W)
        spot = onehot(sub64, plc[pl.ds(a, 1), :])
        low = jnp.broadcast_to(ints[0, pl.ds(a, 1), :], (16, W))
        for q in range(8):
            pick = jnp.where(low == q, 1.0, 0.0).astype(BF16)
            plo[q * CAP : (q + 1) * CAP, col] = spot * jnp.concatenate([pick] * 4, axis=0)
        return 0

    lax.fori_loop(0, 32, fill_plo, 0, unroll=2)
    turned = jnp.concatenate(
        [(order >> 3).astype(F32), plc[...].astype(F32), jnp.zeros((64, W), F32)], axis=0
    ).T
    for a in range(32):
        hib[a * W : (a + 1) * W, :] = jnp.broadcast_to(turned[:, a : a + 1], (W, W)).astype(BF16)

    pltpu.make_async_copy(tr_hbm, tr, in_sem).wait()

    up = (lax.rem(b + NB - 1, NB), s)
    down = (lax.rem(b + 1, NB), s)
    left = (b, lax.rem(s + NS - 1, NS))
    right = (b, lax.rem(s + 1, NS))

    def rcopy(src, dst, ss, rs, dev):
        return pltpu.make_async_remote_copy(
            src_ref=src, dst_ref=dst, send_sem=ss, recv_sem=rs, device_id=dev, device_id_type=MESH
        )

    lane8 = lax.broadcasted_iota(I32, (8, W), 1)

    def early_copies():
        return [
            rcopy(eu, vd, vsend.at[0], vrecv.at[0], up),
            rcopy(ed, vu, vsend.at[1], vrecv.at[1], down),
            rcopy(el, vr, vsend.at[2], vrecv.at[2], left),
            rcopy(er, vl, vsend.at[3], vrecv.at[3], right),
        ]

    def early():
        eu[...] = jnp.zeros_like(eu)
        ed[...] = jnp.zeros_like(ed)
        eu[0:1, :] = sm_ref[0:1, :]
        ed[0:1, :] = sm_ref[31:32, :]
        for k in range(4):
            eu[k + 1 : k + 2, :] = lk_ref[k, 0:1, :].astype(F32)
            ed[k + 1 : k + 2, :] = lk_ref[k, 31:32, :].astype(F32)
        eu[5:6, :] = codes[0:1, :].astype(F32)
        eu[6:7, :] = prior_ref[0:1, :]
        ed[5:6, :] = prior_ref[255:256, :]
        columns = [prior_ref[a * 8 : (a + 1) * 8, :] for a in range(32)]
        columns += [sm_ref[a * 8 : (a + 1) * 8, :] for a in range(4)]
        for k in range(4):
            columns += [lk_ref[k, a * 8 : (a + 1) * 8, :].astype(F32) for a in range(4)]
        columns += [codes[a * 8 : (a + 1) * 8, :].astype(F32) for a in range(4)]
        first = jnp.zeros((8, W), F32)
        last = jnp.zeros((8, W), F32)
        for a, tile in enumerate(columns):
            first = jnp.where(lane8 == a, jnp.broadcast_to(tile[:, 0:1], (8, W)), first)
            last = jnp.where(lane8 == a, jnp.broadcast_to(tile[:, W - 1 : W], (8, W)), last)
        el[...] = first
        er[...] = last
        for c in early_copies():
            c.start()

    def stage1_copy(d):
        to = lax.rem(s + d, NS)
        return rcopy(
            labl.at[pl.ds(to * NB, NB)], r1.at[pl.ds(s * NB, NB)], lsend, lrecv, (b, to)
        )

    def labels_stage1():
        node1 = node_ref[...] + 1
        ints[2] = node1 >> 6
        ints[3] = node1 & 63

        def scale(a, _):
            col = pl.ds(pl.multiple_of(a * W, W), W)
            block = ot[0:W, col]
            low = ints[3, pl.ds(a, 1), :].astype(F32)
            high = ints[2, pl.ds(a, 1), :].astype(F32)
            low = jnp.broadcast_to(low, (16, W)).astype(BF16)
            high = jnp.broadcast_to(high, (16, W)).astype(BF16)
            ot[W : 2 * W, col] = block * jnp.concatenate([low] * 8, axis=0)
            ot[0:W, col] = block * jnp.concatenate([high] * 8, axis=0)
            return 0

        lax.fori_loop(0, 32, scale, 0, unroll=2)
        spots = jnp.concatenate([plc[...].astype(F32), jnp.zeros((96, W), F32)], axis=0).T
        lane64 = (lax.broadcasted_iota(I32, (W, W), 1) & (CAP - 1)).astype(F32)
        for a in range(32):
            rhs[a * W : (a + 1) * W, 0:W] = jnp.where(
                jnp.broadcast_to(spots[:, a : a + 1], (W, W)) == lane64, 1.0, 0.0
            ).astype(BF16)
        out = jnp.dot(ot[...], rhs[:, 0:W], preferred_element_type=F32)
        labl[...] = (out[0:W, :] * 64.0 + out[W : 2 * W, :]).astype(I32)
        r1[pl.ds(pl.multiple_of(s * NB, NB), NB), :] = labl[pl.ds(pl.multiple_of(s * NB, NB), NB), :]

        pl.semaphore_wait(bar, ND - 1)

        def go(d, _):
            stage1_copy(d).start()
            return 0

        lax.fori_loop(1, NS, go, 0)

    def stage2_copy(d):
        to = lax.rem(b + d, NB)
        return rcopy(
            r2.at[pl.ds(to * NS, NS)], ids.at[pl.ds(b * NS, NS)], l2send, l2recv, (to, s)
        )

    def labels_stage2():
        pltpu.make_async_copy(labl.at[pl.ds(0, 7 * NB)], r1.at[pl.ds(0, 7 * NB)], lrecv).wait()
        for t in range(NB):
            r2[t * NS : (t + 1) * NS, :] = r1[pl.ds(t, NS, stride=NB), :]
        mine = pl.ds(pl.multiple_of(b * NS, NS), NS)
        ids[mine, :] = r2[mine, :]

        def go(d, _):
            stage2_copy(d).start()
            return 0

        lax.fori_loop(1, NB, go, 0)

    def trace_copy(i):
        t = lax.rem(me + STRIDE * (i + 1), ND)
        return rcopy(
            sendbuf.at[i], recv.at[i], tsend, trecv.at[i // PER], (t // NS, lax.rem(t, NS))
        )

    def fill_step(j):
        group = hib[...]
        data = tr[...]
        masked = [
            jnp.where(group == jnp.full((ROWS, W), 2 * j + h, I32).astype(F32).astype(BF16), data, jnp.zeros_like(data))
            for h in range(2)
        ]
        out = jnp.dot(plo[...], jnp.concatenate(masked, axis=1), preferred_element_type=F32).astype(BF16)
        for h in range(2):
            sendbuf[pl.ds(PER * j + 8 * h, 8)] = out[:, h * W : (h + 1) * W].reshape(8, CAP, W)

    def dispatch(j, _):
        def go(i, _):
            trace_copy(PER * (j - 1) + i).start()
            return 0

        lax.fori_loop(0, PER, go, 0)
        fill_step(j)

        @pl.when(j == 1)
        def _():
            labels_stage2()

        @pl.when(j == 4)
        def _():
            early()

        return 0

    labels_stage1()
    fill_step(0)
    lax.fori_loop(1, STEPS, dispatch, 0)

    def last(i, _):
        trace_copy(PER * (STEPS - 1) + i).start()
        return 0

    lax.fori_loop(0, PER - 1, last, 0)
    pltpu.make_async_copy(sendbuf.at[ND - 1], recv.at[ND - 1], trecv.at[STEPS - 1]).start()

    pltpu.make_async_copy(r2.at[pl.ds(0, 15 * NS)], ids.at[pl.ds(0, 15 * NS)], l2recv).wait()

    def reorder(i, _):
        src = lax.rem(me - STRIDE * (i + 1) + ND * STRIDE, ND)
        idrel[pl.ds(i, 1), :] = ids[pl.ds(src, 1), :]
        return 0

    lax.fori_loop(0, ND, reorder, 0, unroll=8)
    lane64w = lax.broadcasted_iota(I32, (64, W), 1)
    pairs[...] = jnp.where(lane64w < CAP, ids[pl.ds(0, 64, stride=2), :], ids[pl.ds(1, 64, stride=2), :]) - 1
    idp[...] = jnp.where(lane64w < CAP, idrel[pl.ds(0, 64, stride=2), :], idrel[pl.ds(1, 64, stride=2), :]) - 1
    quarters = jnp.concatenate([(idp[...] >> 10).astype(F32), jnp.zeros((64, W), F32)], axis=0).T
    for a in range(64):
        nhib[a * W : (a + 1) * W, :] = jnp.broadcast_to(quarters[:, a : a + 1], (W, W)).astype(BF16)
    acc[...] = jnp.zeros_like(acc)

    def combine(k, _):
        pltpu.make_async_copy(
            sendbuf.at[pl.ds(0, PER)], recv.at[pl.ds(PER * k, PER)], trecv.at[k]
        ).wait()
        for p in range(8):
            node = idp[pl.ds(8 * k + p, 1), :] & (CLO - 1)
            spot = onehot(sub64, node & 63)
            high = jnp.broadcast_to(node >> 6, (16, W))
            for q in range(16):
                pick = jnp.where(high == q, 1.0, 0.0).astype(BF16)
                qlo[q * CAP : (q + 1) * CAP, p * W : (p + 1) * W] = spot * jnp.concatenate([pick] * 4, axis=0)

        group = nhib[pl.ds(pl.multiple_of(k * CHUNK, CHUNK), CHUNK), :]
        data = recv[pl.ds(PER * k, PER)].reshape(CHUNK, W)
        masked = [
            jnp.where(group == jnp.full((CHUNK, W), h, BF16), data, jnp.zeros_like(data)) for h in range(4)
        ]
        acc[...] += jnp.dot(qlo[...], jnp.concatenate(masked, axis=1), preferred_element_type=F32)
        return 0

    lax.fori_loop(0, STEPS, combine, 0)

    lane1 = lax.broadcasted_iota(I32, (16, W), 1)
    weights = jnp.zeros((16, W), F32)
    total = jnp.float32(0.0)
    for c in range(16):
        wc = cw_ref[c].astype(F32)
        total = total + wc
        weights = jnp.where((lane1 >> 3) == c, wc, weights)
    weights = jnp.where((lane1 & 7) < 4, weights, 0.0).astype(BF16)
    contract = (((1,), (1,)), ((), ()))
    for h in range(4):
        x = acc[:, h * W : (h + 1) * W]
        prod = x * pltpu.roll(x, W - 4, axis=1)
        coarse = prod.astype(BF16)
        fine = (prod - coarse.astype(F32)).astype(BF16)
        d = lax.dot_general(weights, coarse, contract, preferred_element_type=F32)
        d = d + lax.dot_general(weights, fine, contract, preferred_element_type=F32)
        for q in range(8):
            sheet[8 * h + q : 8 * h + q + 1, :] = d[0:1, q * W : (q + 1) * W]
    sheet[...] = sheet[...] / total

    upleft = (lax.rem(b + NB - 1, NB), lax.rem(s + NS - 1, NS))
    upright = (lax.rem(b + NB - 1, NB), lax.rem(s + 1, NS))
    downleft = (lax.rem(b + 1, NB), lax.rem(s + NS - 1, NS))
    downright = (lax.rem(b + 1, NB), lax.rem(s + 1, NS))
    top = sheet.at[pl.ds(0, 8)]
    bottom = sheet.at[pl.ds(24, 8)]
    swaps = [
        rcopy(top, ends.at[5], hsend.at[5], hrecv.at[5], upleft),
        rcopy(top, ends.at[4], hsend.at[4], hrecv.at[4], upright),
        rcopy(bottom, ends.at[3], hsend.at[3], hrecv.at[3], downleft),
        rcopy(bottom, ends.at[2], hsend.at[2], hrecv.at[2], downright),
        rcopy(top, ends.at[1], hsend.at[1], hrecv.at[1], up),
        rcopy(bottom, ends.at[0], hsend.at[0], hrecv.at[0], down),
        rcopy(sheet, sides.at[1], hsend.at[6], hrecv.at[6], left),
        rcopy(sheet, sides.at[0], hsend.at[7], hrecv.at[7], right),
    ]
    for c in swaps:
        c.start()
    row32 = lax.broadcasted_iota(I32, (32, W), 0)
    lane32 = lax.broadcasted_iota(I32, (32, W), 1)
    lane1r = lax.broadcasted_iota(I32, (1, W), 1)
    smooth = sm_ref[...]
    link = [lk_ref[i].astype(F32) for i in range(4)]
    no_up, no_down, no_left, no_right = b == 0, b == NB - 1, s == 0, s == NS - 1

    def relax(v, smooth, link, above, below, before, after):
        beside = link[0] * above + link[1] * below + link[2] * before + link[3] * after
        return (v + smooth * beside) / (1.0 + smooth * (link[0] + link[1] + link[2] + link[3]))

    def column(tile, k):
        parts = [jnp.broadcast_to(tile[:, 32 + 4 * k + t : 33 + 4 * k + t], (8, W)) for t in range(4)]
        return jnp.concatenate(parts, axis=0)

    for c in early_copies():
        c.wait()
    coef_left = [column(vl[...], k) for k in range(5)]
    coef_right = [column(vr[...], k) for k in range(5)]
    g = sheet[...]
    for c in swaps:
        c.wait()
    gu6 = jnp.where(no_up, 0.0, ends[0, 6:7, :])
    gu7 = jnp.where(no_up, 0.0, ends[0, 7:8, :])
    gd0 = jnp.where(no_down, 0.0, ends[1, 0:1, :])
    gd1 = jnp.where(no_down, 0.0, ends[1, 1:2, :])
    gul = jnp.where(no_up | no_left, 0.0, ends[2, 7:8, :])
    gur = jnp.where(no_up | no_right, 0.0, ends[3, 7:8, :])
    gdl = jnp.where(no_down | no_left, 0.0, ends[4, 0:1, :])
    gdr = jnp.where(no_down | no_right, 0.0, ends[5, 0:1, :])
    gl = jnp.where(no_left, 0.0, sides[0])
    gr = jnp.where(no_right, 0.0, sides[1])

    def shifted(v, above, below, before, after):
        return (
            jnp.where(row32 == 0, above, pltpu.roll(v, 1, axis=0)),
            jnp.where(row32 == 31, below, pltpu.roll(v, 31, axis=0)),
            jnp.where(lane32 == 0, pltpu.roll(before, 1, axis=1), pltpu.roll(v, 1, axis=1)),
            jnp.where(lane32 == W - 1, pltpu.roll(after, W - 1, axis=1), pltpu.roll(v, W - 1, axis=1)),
        )

    def shifted_row(v, before, after):
        return (
            jnp.where(lane1r == 0, pltpu.roll(before, 1, axis=1), pltpu.roll(v, 1, axis=1)),
            jnp.where(lane1r == W - 1, pltpu.roll(after, W - 1, axis=1), pltpu.roll(v, W - 1, axis=1)),
        )

    one = relax(g, smooth, link, *shifted(g, gu7, gd0, gl, gr))
    one_up = relax(
        gu7, vu[0:1, :], [vu[k : k + 1, :] for k in range(1, 5)], gu6, g[0:1, :], *shifted_row(gu7, gul, gur)
    )
    one_down = relax(
        gd0, vd[0:1, :], [vd[k : k + 1, :] for k in range(1, 5)], g[31:32, :], gd1, *shifted_row(gd0, gdl, gdr)
    )
    one_left = relax(gl, coef_left[0], coef_left[1:], *shifted(gl, gul, gdl, gl, g))
    one_right = relax(gr, coef_right[0], coef_right[1:], *shifted(gr, gur, gdr, g, gr))
    one_up = jnp.where(no_up, 0.0, one_up)
    one_down = jnp.where(no_down, 0.0, one_down)
    one_left = jnp.where(no_left, 0.0, one_left)
    one_right = jnp.where(no_right, 0.0, one_right)
    beside = shifted(one, one_up, one_down, one_left, one_right)
    sumside = link[0] * beside[0] + link[1] * beside[1] + link[2] * beside[2] + link[3] * beside[3]
    two = (g + smooth * sumside) / (1.0 + smooth * (link[0] + link[1] + link[2] + link[3]))
    vtwo[...] = two
    sm_out[...] = two

    def answer(t, _):
        rows = pl.ds(pl.multiple_of(t * 8, 8), 8)
        node = pairs[rows, :]
        ans[rows, :] = lookup(vtwo, 32, node >> 7, node & (W - 1))
        return 0

    lax.fori_loop(0, 8, answer, 0)
    pair = ans[...]
    msg[pl.ds(0, 64, stride=8), :] = pair
    msg[pl.ds(1, 64, stride=8), :] = pltpu.roll(pair, 60, axis=0)
    msg[pl.ds(2, 64, stride=8), :] = jnp.where(
        lane64w < CAP, pltpu.roll(pair, 63, axis=0), pltpu.roll(pair, 1, axis=0)
    )
    core = lax.rem(s, 2)
    chip = b * 4 + s // 2

    far = sorted(range(1, 64), key=lambda o: -sum(min(d, 4 - d) for d in (o >> 4, (o >> 2) & 3, o & 3)))
    cz, cx, cy = b >> 2, b & 3, s >> 1
    for o in far:
        tb = (((cz + (o >> 4)) & 3) << 2) + ((cx + ((o >> 2) & 3)) & 3)
        ty = (cy + (o & 3)) & 3
        rcopy(
            msg.at[pl.ds((tb * 4 + ty) * 8, 8)], back.at[pl.ds(chip * 8, 8)], asend, arecv, (tb, 2 * ty + core)
        ).start()
    here = pl.ds(pl.multiple_of(chip * 8, 8), 8)
    back[here, :] = msg[here, :]
    pltpu.make_async_copy(msg.at[pl.ds(0, 63 * 8)], back.at[pl.ds(0, 63 * 8)], arecv).wait()
    for k in range(3):
        mine3[k] = back[pl.ds(k, 64, stride=8), :]
    swap = rcopy(mine3, other3, csend, crecv, (b, s + 1 - 2 * core))
    swap.start()
    swap.wait()
    def halves(k, half):
        own_part, other_part = mine3[k], other3[k]
        even = jnp.where(core == 0, own_part, other_part)
        odd = jnp.where(core == 0, other_part, own_part)
        even = jnp.where(half == 0, even, pltpu.roll(even, CAP, axis=1))
        odd = jnp.where(half == 1, odd, pltpu.roll(odd, CAP, axis=1))
        return jnp.where(lane64w < CAP, even, odd)

    partner_table = halves(0, 1 - core)
    far_table = halves(2, 1 - core)
    tables[0] = halves(0, core)
    tables[1] = halves(1, core)
    tables[2] = jnp.where(core == 0, far_table, partner_table)
    tables[3] = jnp.where(core == 0, partner_table, far_table)

    def answered(k, code):
        return lookup(tables.at[k], 64, code >> 7, code & (W - 1))

    shift = jnp.concatenate([answered(0, codes[a * 8 : (a + 1) * 8, :]) for a in range(4)], axis=0)
    shift_down = answered(1, vd[...].astype(I32))[5:6, :]
    lanes_late = lane8 < 4
    edge_left = vl[...]
    edge_right = vr[...]
    edge_left = edge_left + jnp.where(
        lanes_late, pltpu.roll(answered(2, edge_left.astype(I32)), W - 52, axis=1), 0.0
    )
    edge_right = edge_right + jnp.where(
        lanes_late, pltpu.roll(answered(3, edge_right.astype(I32)), W - 52, axis=1), 0.0
    )
    x = jnp.concatenate([prior_ref[0:32, :] + shift, prior_ref[32:256, :]], axis=0)
    before = jnp.concatenate([jnp.broadcast_to(edge_left[:, a : a + 1], (8, W)) for a in range(32)], axis=0)
    after = jnp.concatenate([jnp.broadcast_to(edge_right[:, a : a + 1], (8, W)) for a in range(32)], axis=0)
    before = jnp.where(no_left, 0.0, before)
    after = jnp.where(no_right, 0.0, after)
    above = jnp.where(no_up, 0.0, vu[5:6, :])
    below = jnp.where(no_down, 0.0, vd[6:7, :] + shift_down)
    row256 = lax.broadcasted_iota(I32, (256, W), 0)
    lane256 = lax.broadcasted_iota(I32, (256, W), 1)
    above = jnp.where(row256 == 0, above, pltpu.roll(x, 1, axis=0))
    below = jnp.where(row256 == 255, below, pltpu.roll(x, 255, axis=0))
    before = jnp.where(lane256 == 0, before, pltpu.roll(x, 1, axis=1))
    after = jnp.where(lane256 == W - 1, after, pltpu.roll(x, W - 1, axis=1))
    stiff = st_ref[...]
    mv_out[...] = (stiff * x + (above + below + before + after)) / (stiff + 4.0)

    pltpu.make_async_copy(sendbuf.at[pl.ds(0, ND - 1)], recv.at[pl.ds(0, ND - 1)], tsend).wait()
    pltpu.make_async_copy(labl.at[pl.ds(0, 7 * NB)], r1.at[pl.ds(0, 7 * NB)], lsend).wait()
    pltpu.make_async_copy(r2.at[pl.ds(0, 15 * NS)], ids.at[pl.ds(0, 15 * NS)], l2send).wait()
    pltpu.make_async_copy(msg.at[pl.ds(0, 63 * 8)], back.at[pl.ds(0, 63 * 8)], asend).wait()


def local(traces, owner, patch_node, case_weights, smoothing, links, prior, stiffness):
    vmem = pl.BlockSpec(memory_space=pltpu.VMEM)
    V = pltpu.VMEM
    dma = pltpu.SemaphoreType.DMA
    return pl.pallas_call(
        kernel,
        out_shape=(
            jax.ShapeDtypeStruct((32, W), F32),
            jax.ShapeDtypeStruct((256, W), F32),
        ),
        in_specs=[pl.BlockSpec(memory_space=pl.ANY), vmem, vmem, pl.BlockSpec(memory_space=pltpu.SMEM)] + [vmem] * 4,
        out_specs=(vmem, vmem),
        scratch_shapes=[
            V((ROWS, W), BF16),
            V((2 * W, ROWS), BF16),
            V((DLO, ROWS), BF16),
            V((ROWS, W), BF16),
            V((ROWS, 2 * W), BF16),
            V((ND, CAP, W), BF16),
            V((ND, CAP, W), BF16),
            V((4, 32, W), I32),
            V((32, W), I32),
            V((ND, W), I32),
            V((ND, W), I32),
            V((ND, W), I32),
            V((ND, W), I32),
            V((ND, W), I32),
            V((ND // 2, W), I32),
            V((ND * CAP, W), BF16),
            V((CLO, CHUNK), BF16),
            V((CLO, 4 * W), F32),
            V((32, W), F32),
            V((32, W), F32),
            V((2, 32, W), F32),
            V((6, 8, W), F32),
            V((ND // 2, W), I32),
            V((ND // 2, W), F32),
            V((ND * 4, W), F32),
            V((ND * 4, W), F32),
            V((3, ND // 2, W), F32),
            V((3, ND // 2, W), F32),
            V((4, ND // 2, W), F32),
            V((32, W), I32),
            V((8, W), F32),
            V((8, W), F32),
            V((8, W), F32),
            V((8, W), F32),
            V((8, W), F32),
            V((8, W), F32),
            V((8, W), F32),
            V((8, W), F32),
            dma, dma, dma((STEPS,)), dma, dma, dma, dma, dma((8,)), dma((8,)), dma, dma, dma, dma, dma((4,)), dma((4,)),
        ],
        compiler_params=pltpu.CompilerParams(
            collective_id=0, has_side_effects=True, vmem_limit_bytes=56 << 20
        ),
    )(
        traces, owner.reshape(32, W), patch_node.reshape(32, W), case_weights, smoothing, links, prior, stiffness
    )


def solution(mesh):
    in_specs = (
        P(("brick", "slab"), None),
        P(("brick", "slab"), None),
        P(("brick", "slab")),
        P(),
        P("brick", "slab"),
        P(None, "brick", "slab"),
        P("brick", "slab"),
        P("brick", "slab"),
    )
    out_specs = (P("brick", "slab"), P("brick", "slab"))
    return jax.shard_map(local, mesh=mesh, in_specs=in_specs, out_specs=out_specs, check_vma=False)
```

```python
import functools

import jax
import jax.numpy as jnp
from jax import lax
from jax.experimental import pallas as pl
from jax.experimental.pallas import tpu as pltpu
from jax.sharding import PartitionSpec as P

MESH = pl.DeviceIdType.MESH
F32 = jnp.float32
BF16 = jnp.bfloat16
I32 = jnp.int32

NB = 16
NS = 8
ND = NB * NS
ROWS = 4096
CAP = 64
W = 128
STRIDE = 13
UNSTRIDE = 69
STEPS = 8
PER = ND // STEPS
DLO = 512
CLO = 1024
CHUNK = PER * CAP


def onehot(sub, row):
    return jnp.where(sub == row, 1.0, 0.0).astype(BF16)


def lanes(x, index):
    return jnp.take_along_axis(x, index, axis=1, mode="promise_in_bounds")


def lookup(table, nrows, hi, lo):
    out = jnp.zeros(hi.shape, F32)
    for r in range(nrows):
        row = jnp.broadcast_to(table[r : r + 1, :], (8, W))
        out = jnp.where(hi == r, lanes(row, lo), out)
    return out


def kernel(
    tr_hbm, own_ref, node_ref, cw_ref, sm_ref, lk_ref, prior_ref, st_ref,
    sm_out, mv_out,
    tr, ot, plo, hib, rhs, sendbuf, recv, ints, plc, labl, r1, r2, ids, idrel, idp, nhib,
    qlo, acc, sheet, vtwo, sides, ends, pairs, ans, msg, back, mine3, other3, tables, codes, eu, ed, el, er, vu, vd, vl, vr,
    in_sem, tsend, trecv, lsend, lrecv, l2send, l2recv, hsend, hrecv, asend, arecv, csend, crecv, vsend, vrecv,
):
    b = lax.axis_index("brick")
    s = lax.axis_index("slab")
    me = b * NS + s

    bar = pltpu.get_barrier_semaphore()

    def greet(i, _):
        t = (me + i) & (ND - 1)
        pl.semaphore_signal(bar, inc=1, device_id=(t >> 3, t & (NS - 1)), device_id_type=MESH)
        return 0

    lax.fori_loop(1, ND, greet, 0, unroll=4)
    pltpu.make_async_copy(tr_hbm, tr, in_sem).start()

    own = own_ref[...]
    order = ((own - me + ND) * UNSTRIDE - 1) & (ND - 1)
    slabwise = (own & (NS - 1)) * NB + (own >> 3)
    ints[0] = order & 7
    ints[1] = slabwise
    sub128 = lax.broadcasted_iota(I32, (W, W), 0)

    def fill_ot(a, _):
        col = pl.ds(pl.multiple_of(a * W, W), W)
        ot[0:W, col] = onehot(sub128, ints[1, pl.ds(a, 1), :])
        return 0

    lax.fori_loop(0, 32, fill_ot, 0, unroll=4)
    upper = jnp.where(
        lax.broadcasted_iota(I32, (256, 256), 0) < lax.broadcasted_iota(I32, (256, 256), 1), 1.0, 0.0
    ).astype(BF16)
    carry = jnp.zeros((W, 1), F32)
    for k in range(16):
        block = ot[0:W, k * 256 : (k + 1) * 256]
        blockf = block.astype(F32)
        before = jnp.dot(block, upper, preferred_element_type=F32) + carry
        place = jnp.sum(before * blockf, axis=0, keepdims=True).astype(I32)
        plc[2 * k : 2 * k + 1, :] = place[:, :W]
        plc[2 * k + 1 : 2 * k + 2, :] = place[:, W:]
        carry = before[:, 255:256] + blockf[:, 255:256]

    codes[...] = own * CAP + plc[...]

    sub64 = lax.broadcasted_iota(I32, (CAP, W), 0)

    def fill_plo(a, _):
        col = pl.ds(pl.multiple_of(a * W, W), W)
        spot = onehot(sub64, plc[pl.ds(a, 1), :])
        low = jnp.broadcast_to(ints[0, pl.ds(a, 1), :], (16, W))
        for q in range(8):
            pick = jnp.where(low == q, 1.0, 0.0).astype(BF16)
            plo[q * CAP : (q + 1) * CAP, col] = spot * jnp.concatenate([pick] * 4, axis=0)
        return 0

    lax.fori_loop(0, 32, fill_plo, 0, unroll=2)
    turned = jnp.concatenate(
        [(order >> 3).astype(F32), plc[...].astype(F32), jnp.zeros((64, W), F32)], axis=0
    ).T
    for a in range(32):
        hib[a * W : (a + 1) * W, :] = jnp.broadcast_to(turned[:, a : a + 1], (W, W)).astype(BF16)

    pltpu.make_async_copy(tr_hbm, tr, in_sem).wait()

    up = (lax.rem(b + NB - 1, NB), s)
    down = (lax.rem(b + 1, NB), s)
    left = (b, lax.rem(s + NS - 1, NS))
    right = (b, lax.rem(s + 1, NS))

    def rcopy(src, dst, ss, rs, dev):
        return pltpu.make_async_remote_copy(
            src_ref=src, dst_ref=dst, send_sem=ss, recv_sem=rs, device_id=dev, device_id_type=MESH
        )

    lane8 = lax.broadcasted_iota(I32, (8, W), 1)

    def early_copies():
        return [
            rcopy(eu, vd, vsend.at[0], vrecv.at[0], up),
            rcopy(ed, vu, vsend.at[1], vrecv.at[1], down),
            rcopy(el, vr, vsend.at[2], vrecv.at[2], left),
            rcopy(er, vl, vsend.at[3], vrecv.at[3], right),
        ]

    def early():
        eu[...] = jnp.zeros_like(eu)
        ed[...] = jnp.zeros_like(ed)
        eu[0:1, :] = sm_ref[0:1, :]
        ed[0:1, :] = sm_ref[31:32, :]
        for k in range(4):
            eu[k + 1 : k + 2, :] = lk_ref[k, 0:1, :].astype(F32)
            ed[k + 1 : k + 2, :] = lk_ref[k, 31:32, :].astype(F32)
        eu[5:6, :] = codes[0:1, :].astype(F32)
        eu[6:7, :] = prior_ref[0:1, :]
        ed[5:6, :] = prior_ref[255:256, :]
        columns = [prior_ref[a * 8 : (a + 1) * 8, :] for a in range(32)]
        columns += [sm_ref[a * 8 : (a + 1) * 8, :] for a in range(4)]
        for k in range(4):
            columns += [lk_ref[k, a * 8 : (a + 1) * 8, :].astype(F32) for a in range(4)]
        columns += [codes[a * 8 : (a + 1) * 8, :].astype(F32) for a in range(4)]
        first = jnp.zeros((8, W), F32)
        last = jnp.zeros((8, W), F32)
        for a, tile in enumerate(columns):
            first = jnp.where(lane8 == a, jnp.broadcast_to(tile[:, 0:1], (8, W)), first)
            last = jnp.where(lane8 == a, jnp.broadcast_to(tile[:, W - 1 : W], (8, W)), last)
        el[...] = first
        er[...] = last
        for c in early_copies():
            c.start()

    def stage1_copy(d):
        to = (s + d) & (NS - 1)
        return rcopy(
            labl.at[pl.ds(to * NB, NB)], r1.at[pl.ds(s * NB, NB)], lsend, lrecv, (b, to)
        )

    def labels_stage1():
        node1 = node_ref[...] + 1
        ints[2] = node1 >> 6
        ints[3] = node1 & 63

        def scale(a, _):
            col = pl.ds(pl.multiple_of(a * W, W), W)
            block = ot[0:W, col]
            low = ints[3, pl.ds(a, 1), :].astype(F32)
            high = ints[2, pl.ds(a, 1), :].astype(F32)
            low = jnp.broadcast_to(low, (16, W)).astype(BF16)
            high = jnp.broadcast_to(high, (16, W)).astype(BF16)
            ot[W : 2 * W, col] = block * jnp.concatenate([low] * 8, axis=0)
            ot[0:W, col] = block * jnp.concatenate([high] * 8, axis=0)
            return 0

        lax.fori_loop(0, 32, scale, 0, unroll=2)
        spots = jnp.concatenate([plc[...].astype(F32), jnp.zeros((96, W), F32)], axis=0).T
        lane64 = (lax.broadcasted_iota(I32, (W, W), 1) & (CAP - 1)).astype(F32)
        for a in range(32):
            rhs[a * W : (a + 1) * W, 0:W] = jnp.where(
                jnp.broadcast_to(spots[:, a : a + 1], (W, W)) == lane64, 1.0, 0.0
            ).astype(BF16)
        out = jnp.dot(ot[...], rhs[:, 0:W], preferred_element_type=F32)
        labl[...] = (out[0:W, :] * 64.0 + out[W : 2 * W, :]).astype(I32)
        r1[pl.ds(pl.multiple_of(s * NB, NB), NB), :] = labl[pl.ds(pl.multiple_of(s * NB, NB), NB), :]

        pl.semaphore_wait(bar, ND - 1)

        def go(d, _):
            stage1_copy(d).start()
            return 0

        lax.fori_loop(1, NS, go, 0)

    def stage2_copy(d):
        to = (b + d) & (NB - 1)
        return rcopy(
            r2.at[pl.ds(to * NS, NS)], ids.at[pl.ds(b * NS, NS)], l2send, l2recv, (to, s)
        )

    def labels_stage2():
        pltpu.make_async_copy(labl.at[pl.ds(0, 7 * NB)], r1.at[pl.ds(0, 7 * NB)], lrecv).wait()
        for t in range(NB):
            r2[t * NS : (t + 1) * NS, :] = r1[pl.ds(t, NS, stride=NB), :]
        mine = pl.ds(pl.multiple_of(b * NS, NS), NS)
        ids[mine, :] = r2[mine, :]

        def go(d, _):
            stage2_copy(d).start()
            return 0

        lax.fori_loop(1, NB, go, 0)

    def trace_copy(j, n):
        i = PER * j + n
        t = (me + STRIDE * (i + 1)) & (ND - 1)
        return rcopy(
            sendbuf.at[i], recv.at[i], tsend, trecv.at[j], (t >> 3, t & (NS - 1))
        )

    def fill_step(j):
        group = hib[...]
        data = tr[...]
        masked = [
            jnp.where(group == jnp.full((ROWS, W), 2 * j + h, I32).astype(F32).astype(BF16), data, jnp.zeros_like(data))
            for h in range(2)
        ]
        out = jnp.dot(plo[...], jnp.concatenate(masked, axis=1), preferred_element_type=F32).astype(BF16)
        for h in range(2):
            sendbuf[pl.ds(PER * j + 8 * h, 8)] = out[:, h * W : (h + 1) * W].reshape(8, CAP, W)

    def dispatch(j, _):
        def go(i, _):
            trace_copy(j - 1, i).start()
            return 0

        lax.fori_loop(0, PER, go, 0, unroll=4)
        fill_step(j)

        @pl.when(j == 1)
        def _():
            labels_stage2()

        @pl.when(j == 4)
        def _():
            early()

        return 0

    labels_stage1()
    fill_step(0)
    lax.fori_loop(1, STEPS, dispatch, 0)

    def last(i, _):
        trace_copy(STEPS - 1, i).start()
        return 0

    lax.fori_loop(0, PER - 1, last, 0, unroll=5)
    pltpu.make_async_copy(sendbuf.at[ND - 1], recv.at[ND - 1], trecv.at[STEPS - 1]).start()

    pltpu.make_async_copy(r2.at[pl.ds(0, 15 * NS)], ids.at[pl.ds(0, 15 * NS)], l2recv).wait()

    def reorder(i, _):
        src = (me - STRIDE * (i + 1) + ND * STRIDE) & (ND - 1)
        idrel[pl.ds(i, 1), :] = ids[pl.ds(src, 1), :]
        return 0

    lax.fori_loop(0, ND, reorder, 0, unroll=8)
    lane64w = lax.broadcasted_iota(I32, (64, W), 1)
    pairs[...] = jnp.where(lane64w < CAP, ids[pl.ds(0, 64, stride=2), :], ids[pl.ds(1, 64, stride=2), :]) - 1
    idp[...] = jnp.where(lane64w < CAP, idrel[pl.ds(0, 64, stride=2), :], idrel[pl.ds(1, 64, stride=2), :]) - 1
    quarters = jnp.concatenate([(idp[...] >> 10).astype(F32), jnp.zeros((64, W), F32)], axis=0).T
    for a in range(64):
        nhib[a * W : (a + 1) * W, :] = jnp.broadcast_to(quarters[:, a : a + 1], (W, W)).astype(BF16)
    acc[...] = jnp.zeros_like(acc)

    def combine(k, _):
        pltpu.make_async_copy(
            sendbuf.at[pl.ds(0, PER)], recv.at[pl.ds(PER * k, PER)], trecv.at[k]
        ).wait()
        for p in range(8):
            node = idp[pl.ds(8 * k + p, 1), :] & (CLO - 1)
            spot = onehot(sub64, node & 63)
            high = jnp.broadcast_to(node >> 6, (16, W))
            for q in range(16):
                pick = jnp.where(high == q, 1.0, 0.0).astype(BF16)
                qlo[q * CAP : (q + 1) * CAP, p * W : (p + 1) * W] = spot * jnp.concatenate([pick] * 4, axis=0)

        group = nhib[pl.ds(pl.multiple_of(k * CHUNK, CHUNK), CHUNK), :]
        data = recv[pl.ds(PER * k, PER)].reshape(CHUNK, W)
        masked = [
            jnp.where(group == jnp.full((CHUNK, W), h, BF16), data, jnp.zeros_like(data)) for h in range(4)
        ]
        acc[...] += jnp.dot(qlo[...], jnp.concatenate(masked, axis=1), preferred_element_type=F32)
        return 0

    lax.fori_loop(0, STEPS, combine, 0)

    lane1 = lax.broadcasted_iota(I32, (16, W), 1)
    weights = jnp.zeros((16, W), F32)
    total = jnp.float32(0.0)
    for c in range(16):
        wc = cw_ref[c].astype(F32)
        total = total + wc
        weights = jnp.where((lane1 >> 3) == c, wc, weights)
    weights = jnp.where((lane1 & 7) < 4, weights, 0.0).astype(BF16)
    contract = (((1,), (1,)), ((), ()))
    for h in range(4):
        x = acc[:, h * W : (h + 1) * W]
        prod = x * pltpu.roll(x, W - 4, axis=1)
        coarse = prod.astype(BF16)
        fine = (prod - coarse.astype(F32)).astype(BF16)
        d = lax.dot_general(weights, coarse, contract, preferred_element_type=F32)
        d = d + lax.dot_general(weights, fine, contract, preferred_element_type=F32)
        for q in range(8):
            sheet[8 * h + q : 8 * h + q + 1, :] = d[0:1, q * W : (q + 1) * W]
    sheet[...] = sheet[...] / total

    upleft = (lax.rem(b + NB - 1, NB), lax.rem(s + NS - 1, NS))
    upright = (lax.rem(b + NB - 1, NB), lax.rem(s + 1, NS))
    downleft = (lax.rem(b + 1, NB), lax.rem(s + NS - 1, NS))
    downright = (lax.rem(b + 1, NB), lax.rem(s + 1, NS))
    top = sheet.at[pl.ds(0, 8)]
    bottom = sheet.at[pl.ds(24, 8)]
    swaps = [
        rcopy(top, ends.at[5], hsend.at[5], hrecv.at[5], upleft),
        rcopy(top, ends.at[4], hsend.at[4], hrecv.at[4], upright),
        rcopy(bottom, ends.at[3], hsend.at[3], hrecv.at[3], downleft),
        rcopy(bottom, ends.at[2], hsend.at[2], hrecv.at[2], downright),
        rcopy(top, ends.at[1], hsend.at[1], hrecv.at[1], up),
        rcopy(bottom, ends.at[0], hsend.at[0], hrecv.at[0], down),
        rcopy(sheet, sides.at[1], hsend.at[6], hrecv.at[6], left),
        rcopy(sheet, sides.at[0], hsend.at[7], hrecv.at[7], right),
    ]
    for c in swaps:
        c.start()
    row32 = lax.broadcasted_iota(I32, (32, W), 0)
    lane32 = lax.broadcasted_iota(I32, (32, W), 1)
    lane1r = lax.broadcasted_iota(I32, (1, W), 1)
    smooth = sm_ref[...]
    link = [lk_ref[i].astype(F32) for i in range(4)]
    no_up, no_down, no_left, no_right = b == 0, b == NB - 1, s == 0, s == NS - 1

    def relax(v, smooth, link, above, below, before, after):
        beside = link[0] * above + link[1] * below + link[2] * before + link[3] * after
        return (v + smooth * beside) / (1.0 + smooth * (link[0] + link[1] + link[2] + link[3]))

    def column(tile, k):
        parts = [jnp.broadcast_to(tile[:, 32 + 4 * k + t : 33 + 4 * k + t], (8, W)) for t in range(4)]
        return jnp.concatenate(parts, axis=0)

    for c in early_copies():
        c.wait()
    coef_left = [column(vl[...], k) for k in range(5)]
    coef_right = [column(vr[...], k) for k in range(5)]
    g = sheet[...]
    for c in swaps:
        c.wait()
    gu6 = jnp.where(no_up, 0.0, ends[0, 6:7, :])
    gu7 = jnp.where(no_up, 0.0, ends[0, 7:8, :])
    gd0 = jnp.where(no_down, 0.0, ends[1, 0:1, :])
    gd1 = jnp.where(no_down, 0.0, ends[1, 1:2, :])
    gul = jnp.where(no_up | no_left, 0.0, ends[2, 7:8, :])
    gur = jnp.where(no_up | no_right, 0.0, ends[3, 7:8, :])
    gdl = jnp.where(no_down | no_left, 0.0, ends[4, 0:1, :])
    gdr = jnp.where(no_down | no_right, 0.0, ends[5, 0:1, :])
    gl = jnp.where(no_left, 0.0, sides[0])
    gr = jnp.where(no_right, 0.0, sides[1])

    def shifted(v, above, below, before, after):
        return (
            jnp.where(row32 == 0, above, pltpu.roll(v, 1, axis=0)),
            jnp.where(row32 == 31, below, pltpu.roll(v, 31, axis=0)),
            jnp.where(lane32 == 0, pltpu.roll(before, 1, axis=1), pltpu.roll(v, 1, axis=1)),
            jnp.where(lane32 == W - 1, pltpu.roll(after, W - 1, axis=1), pltpu.roll(v, W - 1, axis=1)),
        )

    def shifted_row(v, before, after):
        return (
            jnp.where(lane1r == 0, pltpu.roll(before, 1, axis=1), pltpu.roll(v, 1, axis=1)),
            jnp.where(lane1r == W - 1, pltpu.roll(after, W - 1, axis=1), pltpu.roll(v, W - 1, axis=1)),
        )

    one = relax(g, smooth, link, *shifted(g, gu7, gd0, gl, gr))
    one_up = relax(
        gu7, vu[0:1, :], [vu[k : k + 1, :] for k in range(1, 5)], gu6, g[0:1, :], *shifted_row(gu7, gul, gur)
    )
    one_down = relax(
        gd0, vd[0:1, :], [vd[k : k + 1, :] for k in range(1, 5)], g[31:32, :], gd1, *shifted_row(gd0, gdl, gdr)
    )
    one_left = relax(gl, coef_left[0], coef_left[1:], *shifted(gl, gul, gdl, gl, g))
    one_right = relax(gr, coef_right[0], coef_right[1:], *shifted(gr, gur, gdr, g, gr))
    one_up = jnp.where(no_up, 0.0, one_up)
    one_down = jnp.where(no_down, 0.0, one_down)
    one_left = jnp.where(no_left, 0.0, one_left)
    one_right = jnp.where(no_right, 0.0, one_right)
    beside = shifted(one, one_up, one_down, one_left, one_right)
    sumside = link[0] * beside[0] + link[1] * beside[1] + link[2] * beside[2] + link[3] * beside[3]
    two = (g + smooth * sumside) / (1.0 + smooth * (link[0] + link[1] + link[2] + link[3]))
    vtwo[...] = two
    sm_out[...] = two

    def answer(t, _):
        rows = pl.ds(pl.multiple_of(t * 8, 8), 8)
        node = pairs[rows, :]
        ans[rows, :] = lookup(vtwo, 32, node >> 7, node & (W - 1))
        return 0

    lax.fori_loop(0, 8, answer, 0)
    pair = ans[...]
    msg[pl.ds(0, 64, stride=8), :] = pair
    msg[pl.ds(1, 64, stride=8), :] = pltpu.roll(pair, 60, axis=0)
    msg[pl.ds(2, 64, stride=8), :] = jnp.where(
        lane64w < CAP, pltpu.roll(pair, 63, axis=0), pltpu.roll(pair, 1, axis=0)
    )
    core = lax.rem(s, 2)
    chip = b * 4 + s // 2

    far = sorted(range(1, 64), key=lambda o: -sum(min(d, 4 - d) for d in (o >> 4, (o >> 2) & 3, o & 3)))
    cz, cx, cy = b >> 2, b & 3, s >> 1
    for o in far:
        tb = (((cz + (o >> 4)) & 3) << 2) + ((cx + ((o >> 2) & 3)) & 3)
        ty = (cy + (o & 3)) & 3
        rcopy(
            msg.at[pl.ds((tb * 4 + ty) * 8, 8)], back.at[pl.ds(chip * 8, 8)], asend, arecv, (tb, 2 * ty + core)
        ).start()
    here = pl.ds(pl.multiple_of(chip * 8, 8), 8)
    back[here, :] = msg[here, :]
    pltpu.make_async_copy(msg.at[pl.ds(0, 63 * 8)], back.at[pl.ds(0, 63 * 8)], arecv).wait()
    for k in range(3):
        mine3[k] = back[pl.ds(k, 64, stride=8), :]
    swap = rcopy(mine3, other3, csend, crecv, (b, s + 1 - 2 * core))
    swap.start()
    swap.wait()
    def halves(k, half):
        own_part, other_part = mine3[k], other3[k]
        even = jnp.where(core == 0, own_part, other_part)
        odd = jnp.where(core == 0, other_part, own_part)
        even = jnp.where(half == 0, even, pltpu.roll(even, CAP, axis=1))
        odd = jnp.where(half == 1, odd, pltpu.roll(odd, CAP, axis=1))
        return jnp.where(lane64w < CAP, even, odd)

    partner_table = halves(0, 1 - core)
    far_table = halves(2, 1 - core)
    tables[0] = halves(0, core)
    tables[1] = halves(1, core)
    tables[2] = jnp.where(core == 0, far_table, partner_table)
    tables[3] = jnp.where(core == 0, partner_table, far_table)

    def answered(k, code):
        return lookup(tables.at[k], 64, code >> 7, code & (W - 1))

    shift = jnp.concatenate([answered(0, codes[a * 8 : (a + 1) * 8, :]) for a in range(4)], axis=0)
    shift_down = answered(1, vd[...].astype(I32))[5:6, :]
    lanes_late = lane8 < 4
    edge_left = vl[...]
    edge_right = vr[...]
    edge_left = edge_left + jnp.where(
        lanes_late, pltpu.roll(answered(2, edge_left.astype(I32)), W - 52, axis=1), 0.0
    )
    edge_right = edge_right + jnp.where(
        lanes_late, pltpu.roll(answered(3, edge_right.astype(I32)), W - 52, axis=1), 0.0
    )
    x = jnp.concatenate([prior_ref[0:32, :] + shift, prior_ref[32:256, :]], axis=0)
    before = jnp.concatenate([jnp.broadcast_to(edge_left[:, a : a + 1], (8, W)) for a in range(32)], axis=0)
    after = jnp.concatenate([jnp.broadcast_to(edge_right[:, a : a + 1], (8, W)) for a in range(32)], axis=0)
    before = jnp.where(no_left, 0.0, before)
    after = jnp.where(no_right, 0.0, after)
    above = jnp.where(no_up, 0.0, vu[5:6, :])
    below = jnp.where(no_down, 0.0, vd[6:7, :] + shift_down)
    row256 = lax.broadcasted_iota(I32, (256, W), 0)
    lane256 = lax.broadcasted_iota(I32, (256, W), 1)
    above = jnp.where(row256 == 0, above, pltpu.roll(x, 1, axis=0))
    below = jnp.where(row256 == 255, below, pltpu.roll(x, 255, axis=0))
    before = jnp.where(lane256 == 0, before, pltpu.roll(x, 1, axis=1))
    after = jnp.where(lane256 == W - 1, after, pltpu.roll(x, W - 1, axis=1))
    stiff = st_ref[...]
    mv_out[...] = (stiff * x + (above + below + before + after)) / (stiff + 4.0)

    pltpu.make_async_copy(sendbuf.at[pl.ds(0, ND - 1)], recv.at[pl.ds(0, ND - 1)], tsend).wait()
    pltpu.make_async_copy(labl.at[pl.ds(0, 7 * NB)], r1.at[pl.ds(0, 7 * NB)], lsend).wait()
    pltpu.make_async_copy(r2.at[pl.ds(0, 15 * NS)], ids.at[pl.ds(0, 15 * NS)], l2send).wait()
    pltpu.make_async_copy(msg.at[pl.ds(0, 63 * 8)], back.at[pl.ds(0, 63 * 8)], asend).wait()


def local(traces, owner, patch_node, case_weights, smoothing, links, prior, stiffness):
    vmem = pl.BlockSpec(memory_space=pltpu.VMEM)
    V = pltpu.VMEM
    dma = pltpu.SemaphoreType.DMA
    return pl.pallas_call(
        kernel,
        out_shape=(
            jax.ShapeDtypeStruct((32, W), F32),
            jax.ShapeDtypeStruct((256, W), F32),
        ),
        in_specs=[pl.BlockSpec(memory_space=pl.ANY), vmem, vmem, pl.BlockSpec(memory_space=pltpu.SMEM)] + [vmem] * 4,
        out_specs=(vmem, vmem),
        scratch_shapes=[
            V((ROWS, W), BF16),
            V((2 * W, ROWS), BF16),
            V((DLO, ROWS), BF16),
            V((ROWS, W), BF16),
            V((ROWS, 2 * W), BF16),
            V((ND, CAP, W), BF16),
            V((ND, CAP, W), BF16),
            V((4, 32, W), I32),
            V((32, W), I32),
            V((ND, W), I32),
            V((ND, W), I32),
            V((ND, W), I32),
            V((ND, W), I32),
            V((ND, W), I32),
            V((ND // 2, W), I32),
            V((ND * CAP, W), BF16),
            V((CLO, CHUNK), BF16),
            V((CLO, 4 * W), F32),
            V((32, W), F32),
            V((32, W), F32),
            V((2, 32, W), F32),
            V((6, 8, W), F32),
            V((ND // 2, W), I32),
            V((ND // 2, W), F32),
            V((ND * 4, W), F32),
            V((ND * 4, W), F32),
            V((3, ND // 2, W), F32),
            V((3, ND // 2, W), F32),
            V((4, ND // 2, W), F32),
            V((32, W), I32),
            V((8, W), F32),
            V((8, W), F32),
            V((8, W), F32),
            V((8, W), F32),
            V((8, W), F32),
            V((8, W), F32),
            V((8, W), F32),
            V((8, W), F32),
            dma, dma, dma((STEPS,)), dma, dma, dma, dma, dma((8,)), dma((8,)), dma, dma, dma, dma, dma((4,)), dma((4,)),
        ],
        compiler_params=pltpu.CompilerParams(
            collective_id=0, has_side_effects=True, vmem_limit_bytes=56 << 20
        ),
    )(
        traces, owner.reshape(32, W), patch_node.reshape(32, W), case_weights, smoothing, links, prior, stiffness
    )


def solution(mesh):
    in_specs = (
        P(("brick", "slab"), None),
        P(("brick", "slab"), None),
        P(("brick", "slab")),
        P(),
        P("brick", "slab"),
        P(None, "brick", "slab"),
        P("brick", "slab"),
        P("brick", "slab"),
    )
    out_specs = (P("brick", "slab"), P("brick", "slab"))
    return jax.shard_map(local, mesh=mesh, in_specs=in_specs, out_specs=out_specs, check_vma=False)
```

```python
import functools

import jax
import jax.numpy as jnp
from jax import lax
from jax.experimental import pallas as pl
from jax.experimental.pallas import tpu as pltpu
from jax.sharding import PartitionSpec as P

MESH = pl.DeviceIdType.MESH
F32 = jnp.float32
BF16 = jnp.bfloat16
I32 = jnp.int32

NB = 16
NS = 8
ND = NB * NS
ROWS = 4096
CAP = 64
W = 128
STRIDE = 13
UNSTRIDE = 69
STEPS = 8
PER = ND // STEPS
DLO = 512
CLO = 1024
CHUNK = PER * CAP


def onehot(sub, row):
    return jnp.where(sub == row, 1.0, 0.0).astype(BF16)


def lanes(x, index):
    return jnp.take_along_axis(x, index, axis=1, mode="promise_in_bounds")


def lookup(table, nrows, hi, lo):
    out = jnp.zeros(hi.shape, F32)
    for r in range(nrows):
        row = jnp.broadcast_to(table[r : r + 1, :], (8, W))
        out = jnp.where(hi == r, lanes(row, lo), out)
    return out


def kernel(
    tr_hbm, own_ref, node_ref, cw_ref, sm_ref, lk_ref, prior_ref, st_ref,
    sm_out, mv_out,
    tr, ot, plo, hib, rhs, sendbuf, recv, ints, plc, labl, r1, r2, ids, idrel, idp, nhib,
    qlo, acc, sheet, vtwo, sides, ends, pairs, ans, msg, back, mine3, other3, tables, codes, eu, ed, el, er, vu, vd, vl, vr,
    in_sem, tsend, trecv, lsend, lrecv, l2send, l2recv, hsend, hrecv, asend, arecv, csend, crecv, vsend, vrecv,
):
    b = lax.axis_index("brick")
    s = lax.axis_index("slab")
    me = b * NS + s

    bar = pltpu.get_barrier_semaphore()

    def greet(i, _):
        t = (me + i) & (ND - 1)
        pl.semaphore_signal(bar, inc=1, device_id=(t >> 3, t & (NS - 1)), device_id_type=MESH)
        return 0

    lax.fori_loop(1, ND, greet, 0, unroll=4)
    pltpu.make_async_copy(tr_hbm, tr, in_sem).start()

    own = own_ref[...]
    order = ((own - me + ND) * UNSTRIDE - 1) & (ND - 1)
    slabwise = (own & (NS - 1)) * NB + (own >> 3)
    ints[0] = order & 7
    ints[1] = slabwise
    sub128 = lax.broadcasted_iota(I32, (W, W), 0)

    def fill_ot(a, _):
        col = pl.ds(pl.multiple_of(a * W, W), W)
        ot[0:W, col] = onehot(sub128, ints[1, pl.ds(a, 1), :])
        return 0

    lax.fori_loop(0, 32, fill_ot, 0, unroll=4)
    upper = jnp.where(
        lax.broadcasted_iota(I32, (256, 256), 0) < lax.broadcasted_iota(I32, (256, 256), 1), 1.0, 0.0
    ).astype(BF16)
    carry = jnp.zeros((W, 1), F32)
    for k in range(16):
        block = ot[0:W, k * 256 : (k + 1) * 256]
        blockf = block.astype(F32)
        before = jnp.dot(block, upper, preferred_element_type=F32) + carry
        place = jnp.sum(before * blockf, axis=0, keepdims=True).astype(I32)
        plc[2 * k : 2 * k + 1, :] = place[:, :W]
        plc[2 * k + 1 : 2 * k + 2, :] = place[:, W:]
        carry = before[:, 255:256] + blockf[:, 255:256]

    codes[...] = own * CAP + plc[...]

    sub64 = lax.broadcasted_iota(I32, (CAP, W), 0)

    def fill_plo(a, _):
        col = pl.ds(pl.multiple_of(a * W, W), W)
        spot = onehot(sub64, plc[pl.ds(a, 1), :])
        low = jnp.broadcast_to(ints[0, pl.ds(a, 1), :], (16, W))
        for q in range(8):
            pick = jnp.where(low == q, 1.0, 0.0).astype(BF16)
            plo[q * CAP : (q + 1) * CAP, col] = spot * jnp.concatenate([pick] * 4, axis=0)
        return 0

    lax.fori_loop(0, 32, fill_plo, 0, unroll=2)
    turned = jnp.concatenate(
        [(order >> 3).astype(F32), plc[...].astype(F32), jnp.zeros((64, W), F32)], axis=0
    ).T
    for a in range(32):
        hib[a * W : (a + 1) * W, :] = jnp.broadcast_to(turned[:, a : a + 1], (W, W)).astype(BF16)

    pltpu.make_async_copy(tr_hbm, tr, in_sem).wait()

    up = (lax.rem(b + NB - 1, NB), s)
    down = (lax.rem(b + 1, NB), s)
    left = (b, lax.rem(s + NS - 1, NS))
    right = (b, lax.rem(s + 1, NS))

    def rcopy(src, dst, ss, rs, dev):
        return pltpu.make_async_remote_copy(
            src_ref=src, dst_ref=dst, send_sem=ss, recv_sem=rs, device_id=dev, device_id_type=MESH
        )

    lane8 = lax.broadcasted_iota(I32, (8, W), 1)

    def early_copies():
        return [
            rcopy(eu, vd, vsend.at[0], vrecv.at[0], up),
            rcopy(ed, vu, vsend.at[1], vrecv.at[1], down),
            rcopy(el, vr, vsend.at[2], vrecv.at[2], left),
            rcopy(er, vl, vsend.at[3], vrecv.at[3], right),
        ]

    def early():
        eu[...] = jnp.zeros_like(eu)
        ed[...] = jnp.zeros_like(ed)
        eu[0:1, :] = sm_ref[0:1, :]
        ed[0:1, :] = sm_ref[31:32, :]
        for k in range(4):
            eu[k + 1 : k + 2, :] = lk_ref[k, 0:1, :].astype(F32)
            ed[k + 1 : k + 2, :] = lk_ref[k, 31:32, :].astype(F32)
        eu[5:6, :] = codes[0:1, :].astype(F32)
        eu[6:7, :] = prior_ref[0:1, :]
        ed[5:6, :] = prior_ref[255:256, :]
        columns = [prior_ref[a * 8 : (a + 1) * 8, :] for a in range(32)]
        columns += [sm_ref[a * 8 : (a + 1) * 8, :] for a in range(4)]
        for k in range(4):
            columns += [lk_ref[k, a * 8 : (a + 1) * 8, :].astype(F32) for a in range(4)]
        columns += [codes[a * 8 : (a + 1) * 8, :].astype(F32) for a in range(4)]
        first = jnp.zeros((8, W), F32)
        last = jnp.zeros((8, W), F32)
        for a, tile in enumerate(columns):
            first = jnp.where(lane8 == a, jnp.broadcast_to(tile[:, 0:1], (8, W)), first)
            last = jnp.where(lane8 == a, jnp.broadcast_to(tile[:, W - 1 : W], (8, W)), last)
        el[...] = first
        er[...] = last
        for c in early_copies():
            c.start()

    def stage1_copy(d):
        to = (s + d) & (NS - 1)
        return rcopy(
            labl.at[pl.ds(to * NB, NB)], r1.at[pl.ds(s * NB, NB)], lsend, lrecv, (b, to)
        )

    def labels_stage1():
        node1 = node_ref[...] + 1
        ints[2] = node1 >> 6
        ints[3] = node1 & 63

        def scale(a, _):
            col = pl.ds(pl.multiple_of(a * W, W), W)
            block = ot[0:W, col]
            low = ints[3, pl.ds(a, 1), :].astype(F32)
            high = ints[2, pl.ds(a, 1), :].astype(F32)
            low = jnp.broadcast_to(low, (16, W)).astype(BF16)
            high = jnp.broadcast_to(high, (16, W)).astype(BF16)
            ot[W : 2 * W, col] = block * jnp.concatenate([low] * 8, axis=0)
            ot[0:W, col] = block * jnp.concatenate([high] * 8, axis=0)
            return 0

        lax.fori_loop(0, 32, scale, 0, unroll=2)
        spots = jnp.concatenate([plc[...].astype(F32), jnp.zeros((96, W), F32)], axis=0).T
        lane64 = (lax.broadcasted_iota(I32, (W, W), 1) & (CAP - 1)).astype(F32)
        for a in range(32):
            rhs[a * W : (a + 1) * W, 0:W] = jnp.where(
                jnp.broadcast_to(spots[:, a : a + 1], (W, W)) == lane64, 1.0, 0.0
            ).astype(BF16)
        out = jnp.dot(ot[...], rhs[:, 0:W], preferred_element_type=F32)
        labl[...] = (out[0:W, :] * 64.0 + out[W : 2 * W, :]).astype(I32)
        r1[pl.ds(pl.multiple_of(s * NB, NB), NB), :] = labl[pl.ds(pl.multiple_of(s * NB, NB), NB), :]

        pl.semaphore_wait(bar, ND - 1)

        def go(d, _):
            stage1_copy(d).start()
            return 0

        lax.fori_loop(1, NS, go, 0)

    def stage2_copy(d):
        to = (b + d) & (NB - 1)
        return rcopy(
            r2.at[pl.ds(to * NS, NS)], ids.at[pl.ds(b * NS, NS)], l2send, l2recv, (to, s)
        )

    def labels_stage2():
        pltpu.make_async_copy(labl.at[pl.ds(0, 7 * NB)], r1.at[pl.ds(0, 7 * NB)], lrecv).wait()
        for t in range(NB):
            r2[t * NS : (t + 1) * NS, :] = r1[pl.ds(t, NS, stride=NB), :]
        mine = pl.ds(pl.multiple_of(b * NS, NS), NS)
        ids[mine, :] = r2[mine, :]

        def go(d, _):
            stage2_copy(d).start()
            return 0

        lax.fori_loop(1, NB, go, 0)

    def trace_copy(j, n):
        i = PER * j + n
        t = (me + STRIDE * (i + 1)) & (ND - 1)
        return rcopy(
            sendbuf.at[i], recv.at[i], tsend, trecv.at[j], (t >> 3, t & (NS - 1))
        )

    def fill_step(j):
        group = hib[...]
        data = tr[...]
        masked = [
            jnp.where(group == jnp.full((ROWS, W), 2 * j + h, I32).astype(F32).astype(BF16), data, jnp.zeros_like(data))
            for h in range(2)
        ]
        out = jnp.dot(plo[...], jnp.concatenate(masked, axis=1), preferred_element_type=F32).astype(BF16)
        for h in range(2):
            sendbuf[pl.ds(PER * j + 8 * h, 8)] = out[:, h * W : (h + 1) * W].reshape(8, CAP, W)

    def dispatch(j, _):
        def go(i, _):
            trace_copy(j - 1, i).start()
            return 0

        lax.fori_loop(0, PER, go, 0, unroll=4)
        fill_step(j)

        @pl.when(j == 1)
        def _():
            labels_stage2()

        @pl.when(j == 4)
        def _():
            early()

        return 0

    fill_step(0)
    labels_stage1()
    lax.fori_loop(1, STEPS, dispatch, 0)

    def last(i, _):
        trace_copy(STEPS - 1, i).start()
        return 0

    lax.fori_loop(0, PER - 1, last, 0, unroll=5)
    pltpu.make_async_copy(sendbuf.at[ND - 1], recv.at[ND - 1], trecv.at[STEPS - 1]).start()

    pltpu.make_async_copy(r2.at[pl.ds(0, 15 * NS)], ids.at[pl.ds(0, 15 * NS)], l2recv).wait()

    def reorder(i, _):
        src = (me - STRIDE * (i + 1) + ND * STRIDE) & (ND - 1)
        idrel[pl.ds(i, 1), :] = ids[pl.ds(src, 1), :]
        return 0

    lax.fori_loop(0, ND, reorder, 0, unroll=8)
    lane64w = lax.broadcasted_iota(I32, (64, W), 1)
    pairs[...] = jnp.where(lane64w < CAP, ids[pl.ds(0, 64, stride=2), :], ids[pl.ds(1, 64, stride=2), :]) - 1
    idp[...] = jnp.where(lane64w < CAP, idrel[pl.ds(0, 64, stride=2), :], idrel[pl.ds(1, 64, stride=2), :]) - 1
    quarters = jnp.concatenate([(idp[...] >> 10).astype(F32), jnp.zeros((64, W), F32)], axis=0).T
    for a in range(64):
        nhib[a * W : (a + 1) * W, :] = jnp.broadcast_to(quarters[:, a : a + 1], (W, W)).astype(BF16)
    acc[...] = jnp.zeros_like(acc)

    def combine(k, _):
        pltpu.make_async_copy(
            sendbuf.at[pl.ds(0, PER)], recv.at[pl.ds(PER * k, PER)], trecv.at[k]
        ).wait()
        for p in range(8):
            node = idp[pl.ds(8 * k + p, 1), :] & (CLO - 1)
            spot = onehot(sub64, node & 63)
            high = jnp.broadcast_to(node >> 6, (16, W))
            for q in range(16):
                pick = jnp.where(high == q, 1.0, 0.0).astype(BF16)
                qlo[q * CAP : (q + 1) * CAP, p * W : (p + 1) * W] = spot * jnp.concatenate([pick] * 4, axis=0)

        group = nhib[pl.ds(pl.multiple_of(k * CHUNK, CHUNK), CHUNK), :]
        data = recv[pl.ds(PER * k, PER)].reshape(CHUNK, W)
        masked = [
            jnp.where(group == jnp.full((CHUNK, W), h, BF16), data, jnp.zeros_like(data)) for h in range(4)
        ]
        acc[...] += jnp.dot(qlo[...], jnp.concatenate(masked, axis=1), preferred_element_type=F32)
        return 0

    lax.fori_loop(0, STEPS, combine, 0)

    lane1 = lax.broadcasted_iota(I32, (16, W), 1)
    weights = jnp.zeros((16, W), F32)
    total = jnp.float32(0.0)
    for c in range(16):
        wc = cw_ref[c].astype(F32)
        total = total + wc
        weights = jnp.where((lane1 >> 3) == c, wc, weights)
    weights = jnp.where((lane1 & 7) < 4, weights, 0.0).astype(BF16)
    contract = (((1,), (1,)), ((), ()))
    for h in range(4):
        x = acc[:, h * W : (h + 1) * W]
        prod = x * pltpu.roll(x, W - 4, axis=1)
        coarse = prod.astype(BF16)
        fine = (prod - coarse.astype(F32)).astype(BF16)
        d = lax.dot_general(weights, coarse, contract, preferred_element_type=F32)
        d = d + lax.dot_general(weights, fine, contract, preferred_element_type=F32)
        for q in range(8):
            sheet[8 * h + q : 8 * h + q + 1, :] = d[0:1, q * W : (q + 1) * W]
    sheet[...] = sheet[...] / total

    upleft = (lax.rem(b + NB - 1, NB), lax.rem(s + NS - 1, NS))
    upright = (lax.rem(b + NB - 1, NB), lax.rem(s + 1, NS))
    downleft = (lax.rem(b + 1, NB), lax.rem(s + NS - 1, NS))
    downright = (lax.rem(b + 1, NB), lax.rem(s + 1, NS))
    top = sheet.at[pl.ds(0, 8)]
    bottom = sheet.at[pl.ds(24, 8)]
    swaps = [
        rcopy(top, ends.at[5], hsend.at[5], hrecv.at[5], upleft),
        rcopy(top, ends.at[4], hsend.at[4], hrecv.at[4], upright),
        rcopy(bottom, ends.at[3], hsend.at[3], hrecv.at[3], downleft),
        rcopy(bottom, ends.at[2], hsend.at[2], hrecv.at[2], downright),
        rcopy(top, ends.at[1], hsend.at[1], hrecv.at[1], up),
        rcopy(bottom, ends.at[0], hsend.at[0], hrecv.at[0], down),
        rcopy(sheet, sides.at[1], hsend.at[6], hrecv.at[6], left),
        rcopy(sheet, sides.at[0], hsend.at[7], hrecv.at[7], right),
    ]
    for c in swaps:
        c.start()
    row32 = lax.broadcasted_iota(I32, (32, W), 0)
    lane32 = lax.broadcasted_iota(I32, (32, W), 1)
    lane1r = lax.broadcasted_iota(I32, (1, W), 1)
    smooth = sm_ref[...]
    link = [lk_ref[i].astype(F32) for i in range(4)]
    no_up, no_down, no_left, no_right = b == 0, b == NB - 1, s == 0, s == NS - 1

    def relax(v, smooth, link, above, below, before, after):
        beside = link[0] * above + link[1] * below + link[2] * before + link[3] * after
        return (v + smooth * beside) / (1.0 + smooth * (link[0] + link[1] + link[2] + link[3]))

    def column(tile, k):
        parts = [jnp.broadcast_to(tile[:, 32 + 4 * k + t : 33 + 4 * k + t], (8, W)) for t in range(4)]
        return jnp.concatenate(parts, axis=0)

    for c in early_copies():
        c.wait()
    coef_left = [column(vl[...], k) for k in range(5)]
    coef_right = [column(vr[...], k) for k in range(5)]
    g = sheet[...]
    for c in swaps:
        c.wait()
    gu6 = jnp.where(no_up, 0.0, ends[0, 6:7, :])
    gu7 = jnp.where(no_up, 0.0, ends[0, 7:8, :])
    gd0 = jnp.where(no_down, 0.0, ends[1, 0:1, :])
    gd1 = jnp.where(no_down, 0.0, ends[1, 1:2, :])
    gul = jnp.where(no_up | no_left, 0.0, ends[2, 7:8, :])
    gur = jnp.where(no_up | no_right, 0.0, ends[3, 7:8, :])
    gdl = jnp.where(no_down | no_left, 0.0, ends[4, 0:1, :])
    gdr = jnp.where(no_down | no_right, 0.0, ends[5, 0:1, :])
    gl = jnp.where(no_left, 0.0, sides[0])
    gr = jnp.where(no_right, 0.0, sides[1])

    def shifted(v, above, below, before, after):
        return (
            jnp.where(row32 == 0, above, pltpu.roll(v, 1, axis=0)),
            jnp.where(row32 == 31, below, pltpu.roll(v, 31, axis=0)),
            jnp.where(lane32 == 0, pltpu.roll(before, 1, axis=1), pltpu.roll(v, 1, axis=1)),
            jnp.where(lane32 == W - 1, pltpu.roll(after, W - 1, axis=1), pltpu.roll(v, W - 1, axis=1)),
        )

    def shifted_row(v, before, after):
        return (
            jnp.where(lane1r == 0, pltpu.roll(before, 1, axis=1), pltpu.roll(v, 1, axis=1)),
            jnp.where(lane1r == W - 1, pltpu.roll(after, W - 1, axis=1), pltpu.roll(v, W - 1, axis=1)),
        )

    one = relax(g, smooth, link, *shifted(g, gu7, gd0, gl, gr))
    one_up = relax(
        gu7, vu[0:1, :], [vu[k : k + 1, :] for k in range(1, 5)], gu6, g[0:1, :], *shifted_row(gu7, gul, gur)
    )
    one_down = relax(
        gd0, vd[0:1, :], [vd[k : k + 1, :] for k in range(1, 5)], g[31:32, :], gd1, *shifted_row(gd0, gdl, gdr)
    )
    one_left = relax(gl, coef_left[0], coef_left[1:], *shifted(gl, gul, gdl, gl, g))
    one_right = relax(gr, coef_right[0], coef_right[1:], *shifted(gr, gur, gdr, g, gr))
    one_up = jnp.where(no_up, 0.0, one_up)
    one_down = jnp.where(no_down, 0.0, one_down)
    one_left = jnp.where(no_left, 0.0, one_left)
    one_right = jnp.where(no_right, 0.0, one_right)
    beside = shifted(one, one_up, one_down, one_left, one_right)
    sumside = link[0] * beside[0] + link[1] * beside[1] + link[2] * beside[2] + link[3] * beside[3]
    two = (g + smooth * sumside) / (1.0 + smooth * (link[0] + link[1] + link[2] + link[3]))
    vtwo[...] = two
    sm_out[...] = two

    def answer(t, _):
        rows = pl.ds(pl.multiple_of(t * 8, 8), 8)
        node = pairs[rows, :]
        ans[rows, :] = lookup(vtwo, 32, node >> 7, node & (W - 1))
        return 0

    lax.fori_loop(0, 8, answer, 0)
    pair = ans[...]
    msg[pl.ds(0, 64, stride=8), :] = pair
    msg[pl.ds(1, 64, stride=8), :] = pltpu.roll(pair, 60, axis=0)
    msg[pl.ds(2, 64, stride=8), :] = jnp.where(
        lane64w < CAP, pltpu.roll(pair, 63, axis=0), pltpu.roll(pair, 1, axis=0)
    )
    core = lax.rem(s, 2)
    chip = b * 4 + s // 2

    far = sorted(range(1, 64), key=lambda o: -sum(min(d, 4 - d) for d in (o >> 4, (o >> 2) & 3, o & 3)))
    cz, cx, cy = b >> 2, b & 3, s >> 1
    for o in far:
        tb = (((cz + (o >> 4)) & 3) << 2) + ((cx + ((o >> 2) & 3)) & 3)
        ty = (cy + (o & 3)) & 3
        rcopy(
            msg.at[pl.ds((tb * 4 + ty) * 8, 8)], back.at[pl.ds(chip * 8, 8)], asend, arecv, (tb, 2 * ty + core)
        ).start()
    here = pl.ds(pl.multiple_of(chip * 8, 8), 8)
    back[here, :] = msg[here, :]
    pltpu.make_async_copy(msg.at[pl.ds(0, 63 * 8)], back.at[pl.ds(0, 63 * 8)], arecv).wait()
    for k in range(3):
        mine3[k] = back[pl.ds(k, 64, stride=8), :]
    swap = rcopy(mine3, other3, csend, crecv, (b, s + 1 - 2 * core))
    swap.start()
    swap.wait()
    def halves(k, half):
        own_part, other_part = mine3[k], other3[k]
        even = jnp.where(core == 0, own_part, other_part)
        odd = jnp.where(core == 0, other_part, own_part)
        even = jnp.where(half == 0, even, pltpu.roll(even, CAP, axis=1))
        odd = jnp.where(half == 1, odd, pltpu.roll(odd, CAP, axis=1))
        return jnp.where(lane64w < CAP, even, odd)

    partner_table = halves(0, 1 - core)
    far_table = halves(2, 1 - core)
    tables[0] = halves(0, core)
    tables[1] = halves(1, core)
    tables[2] = jnp.where(core == 0, far_table, partner_table)
    tables[3] = jnp.where(core == 0, partner_table, far_table)

    def answered(k, code):
        return lookup(tables.at[k], 64, code >> 7, code & (W - 1))

    shift = jnp.concatenate([answered(0, codes[a * 8 : (a + 1) * 8, :]) for a in range(4)], axis=0)
    shift_down = answered(1, vd[...].astype(I32))[5:6, :]
    lanes_late = lane8 < 4
    edge_left = vl[...]
    edge_right = vr[...]
    edge_left = edge_left + jnp.where(
        lanes_late, pltpu.roll(answered(2, edge_left.astype(I32)), W - 52, axis=1), 0.0
    )
    edge_right = edge_right + jnp.where(
        lanes_late, pltpu.roll(answered(3, edge_right.astype(I32)), W - 52, axis=1), 0.0
    )
    x = jnp.concatenate([prior_ref[0:32, :] + shift, prior_ref[32:256, :]], axis=0)
    before = jnp.concatenate([jnp.broadcast_to(edge_left[:, a : a + 1], (8, W)) for a in range(32)], axis=0)
    after = jnp.concatenate([jnp.broadcast_to(edge_right[:, a : a + 1], (8, W)) for a in range(32)], axis=0)
    before = jnp.where(no_left, 0.0, before)
    after = jnp.where(no_right, 0.0, after)
    above = jnp.where(no_up, 0.0, vu[5:6, :])
    below = jnp.where(no_down, 0.0, vd[6:7, :] + shift_down)
    row256 = lax.broadcasted_iota(I32, (256, W), 0)
    lane256 = lax.broadcasted_iota(I32, (256, W), 1)
    above = jnp.where(row256 == 0, above, pltpu.roll(x, 1, axis=0))
    below = jnp.where(row256 == 255, below, pltpu.roll(x, 255, axis=0))
    before = jnp.where(lane256 == 0, before, pltpu.roll(x, 1, axis=1))
    after = jnp.where(lane256 == W - 1, after, pltpu.roll(x, W - 1, axis=1))
    stiff = st_ref[...]
    mv_out[...] = (stiff * x + (above + below + before + after)) / (stiff + 4.0)

    pltpu.make_async_copy(sendbuf.at[pl.ds(0, ND - 1)], recv.at[pl.ds(0, ND - 1)], tsend).wait()
    pltpu.make_async_copy(labl.at[pl.ds(0, 7 * NB)], r1.at[pl.ds(0, 7 * NB)], lsend).wait()
    pltpu.make_async_copy(r2.at[pl.ds(0, 15 * NS)], ids.at[pl.ds(0, 15 * NS)], l2send).wait()
    pltpu.make_async_copy(msg.at[pl.ds(0, 63 * 8)], back.at[pl.ds(0, 63 * 8)], asend).wait()


def local(traces, owner, patch_node, case_weights, smoothing, links, prior, stiffness):
    vmem = pl.BlockSpec(memory_space=pltpu.VMEM)
    V = pltpu.VMEM
    dma = pltpu.SemaphoreType.DMA
    return pl.pallas_call(
        kernel,
        out_shape=(
            jax.ShapeDtypeStruct((32, W), F32),
            jax.ShapeDtypeStruct((256, W), F32),
        ),
        in_specs=[pl.BlockSpec(memory_space=pl.ANY), vmem, vmem, pl.BlockSpec(memory_space=pltpu.SMEM)] + [vmem] * 4,
        out_specs=(vmem, vmem),
        scratch_shapes=[
            V((ROWS, W), BF16),
            V((2 * W, ROWS), BF16),
            V((DLO, ROWS), BF16),
            V((ROWS, W), BF16),
            V((ROWS, 2 * W), BF16),
            V((ND, CAP, W), BF16),
            V((ND, CAP, W), BF16),
            V((4, 32, W), I32),
            V((32, W), I32),
            V((ND, W), I32),
            V((ND, W), I32),
            V((ND, W), I32),
            V((ND, W), I32),
            V((ND, W), I32),
            V((ND // 2, W), I32),
            V((ND * CAP, W), BF16),
            V((CLO, CHUNK), BF16),
            V((CLO, 4 * W), F32),
            V((32, W), F32),
            V((32, W), F32),
            V((2, 32, W), F32),
            V((6, 8, W), F32),
            V((ND // 2, W), I32),
            V((ND // 2, W), F32),
            V((ND * 4, W), F32),
            V((ND * 4, W), F32),
            V((3, ND // 2, W), F32),
            V((3, ND // 2, W), F32),
            V((4, ND // 2, W), F32),
            V((32, W), I32),
            V((8, W), F32),
            V((8, W), F32),
            V((8, W), F32),
            V((8, W), F32),
            V((8, W), F32),
            V((8, W), F32),
            V((8, W), F32),
            V((8, W), F32),
            dma, dma, dma((STEPS,)), dma, dma, dma, dma, dma((8,)), dma((8,)), dma, dma, dma, dma, dma((4,)), dma((4,)),
        ],
        compiler_params=pltpu.CompilerParams(
            collective_id=0, has_side_effects=True, vmem_limit_bytes=56 << 20
        ),
    )(
        traces, owner.reshape(32, W), patch_node.reshape(32, W), case_weights, smoothing, links, prior, stiffness
    )


def solution(mesh):
    in_specs = (
        P(("brick", "slab"), None),
        P(("brick", "slab"), None),
        P(("brick", "slab")),
        P(),
        P("brick", "slab"),
        P(None, "brick", "slab"),
        P("brick", "slab"),
        P("brick", "slab"),
    )
    out_specs = (P("brick", "slab"), P("brick", "slab"))
    return jax.shard_map(local, mesh=mesh, in_specs=in_specs, out_specs=out_specs, check_vma=False)
```
